32 devices in a mesh: dp: 4 (over z), fsdp: 8 (over y, x, core).
Axes of the slice: x: 2, y: 2, z: 4, core: 2. Of those that a mesh axis runs over, the one named last changes fastest.
Arguments:
- qkv: bfloat16 [4, 8, 192, 3, 896], P('dp', 'fsdp'), may hold values from -8 to 8
- grad_out: bfloat16 [4, 8, 192, 896], P('dp', 'fsdp'), may hold values from -6 to 6
- lengths: int32 [4, 8, 3], P(None, 'fsdp'), may hold values from 1 to 128, 192 in all within a row
- moves: int32 [8, 2, 3], P('fsdp'), may hold values from 0 to 3, as said below
- out_weight: bfloat16 [896, 896], P('fsdp'), may hold values from -0.1875 to 0.1875
Outputs:
- home_grad: bfloat16 [4, 8, 192, 3, 896], P('dp', 'fsdp')
- inbox_grad: bfloat16 [4, 8, 128, 3, 896], P('dp', 'fsdp')
- weight_grad: float32 [896, 896], P('fsdp', 'dp')
The draws below stay inside these ranges and needn't reach their ends.
Inputs may be any that keep to these rules, and one draw needn't show every extreme that they name: In each fsdp column the sources of the moves differ from one another, and each destination is (source + 1) mod 4; the clip index is below 3. `lengths`: each device's counts sum to 192.
All inputs are finite; a program needn't handle non-finite values.
Results may differ from the reference program's by a relative error of at most 0.023.
Values may be sent and summed in bfloat16 or wider, within the bound.
A program may use at most 64 MiB of HBM per device.

```python
import math
import jax
import jax.numpy as jnp
import numpy as np
from jax import lax

HEADS = 8
HSIZE = 112
DOUT = 896
TOK_DEV = 192
CLIP_MAX = 128
MOVES = 2
CLIPS_DEV = 3
HD = 896
N_DP = 4
N_FSDP = 8


def draw_qkv(key, part):
    key = jax.random.fold_in(key, 7)
    shape = (N_DP, N_FSDP, TOK_DEV, 3, HEADS * HSIZE)
    whole = jnp.clip(jax.random.normal(key, shape, jnp.float32), -8.0, 8.0)
    return whole.astype(jnp.bfloat16)


def draw_moves(key, part):
    key = jax.random.fold_in(key, 5)
    keys = jax.random.split(key, N_FSDP)

    def one_column(sub):
        order = jax.random.permutation(sub, N_DP)
        which = jax.random.randint(jax.random.fold_in(sub, 1), (MOVES,), 0, CLIPS_DEV)
        sources = order[:MOVES]
        return jnp.stack([sources, (sources + 1) % N_DP, which], axis=1).astype(jnp.int32)
    return jax.vmap(one_column)(keys)


def block_scale(stream_key, extent, cuts, low, largest):
    factor_of, own = 1.0, jax.random.fold_in(stream_key, 6)
    for dim, shards_of in cuts:
        draws = jnp.exp(jax.random.uniform(jax.random.fold_in(own, dim), (shards_of,), jnp.float32, low / len(cuts), largest / len(cuts)))
        factor_of = factor_of * jnp.repeat(draws, extent[dim] // shards_of).reshape([-1 if axis == dim else 1 for axis in range(len(extent))])
    return factor_of


def profile(count, total, reach, skew):
    portions = [(1 << 20) // math.isqrt(rank ** skew) + 1 for rank in range(2, count + 1)]
    spare, given = total - reach - (count - 1), [1] * (count - 1)
    while spare > 0:
        movable = [i for i in range(count - 1) if given[i] < reach]
        mass, remaining = sum([portions[i] for i in movable]), spare
        for i in movable:
            more = min(reach - given[i], max(1, remaining * portions[i] // mass), spare)
            given[i] = given[i] + more
            spare = spare - more
    return np.array([reach] + given)


def uneven(stream_key, amount, total, most, lean):
    if amount == 2:
        one = jax.random.randint(stream_key, (), max(1, total - most), min(most, total - 1) + 1)
        return jnp.stack([one, total - one])
    sizes = jnp.asarray(profile(amount, total, most, lean), jnp.int32)
    pairs = (amount - 1) // 2
    donor, receiver = sizes[1:1 + 2 * pairs:2], sizes[2:2 + 2 * pairs:2]
    room = jnp.minimum(donor - 1, most - receiver)
    shifted = jax.random.randint(jax.random.fold_in(stream_key, 1), (pairs,), 0, 1 << 20) % (room + 1)
    sizes = sizes.at[1:1 + 2 * pairs:2].set(donor - shifted).at[2:2 + 2 * pairs:2].set(receiver + shifted)
    return sizes[jax.random.permutation(jax.random.fold_in(stream_key, 2), amount)]


def centred(key, shape, scale, reach, cuts=(), kind=jnp.bfloat16):
    result = jax.random.normal(key, shape, jnp.float32) * scale
    if len(cuts) > 0:
        result = block_scale(key, shape, cuts, -0.22, 0.18) * result
    return jnp.clip(result, min=-reach, max=reach).astype(kind)


def setup_inputs(seed: int = 0) -> dict:
    seeds = jax.random.split(jax.random.key(seed), 6)
    return {
        "qkv": draw_qkv(jax.random.fold_in(seeds[5], 71), 0),
        "grad_out": centred(seeds[1], (N_DP, N_FSDP, TOK_DEV, DOUT), 1.0, 6.0, ((0, 4), (1, 8))),
        "lengths": jax.vmap(lambda own: uneven(own, CLIPS_DEV, TOK_DEV, CLIP_MAX, 2))(jax.random.split(seeds[2], N_DP * N_FSDP)).reshape((N_DP, N_FSDP, CLIPS_DEV)).astype(jnp.int32),
        "moves": draw_moves(jax.random.fold_in(seeds[5], 71), 0),
        "out_weight": centred(seeds[4], (HD, DOUT), HD ** -0.5, 0.1875, ((0, 8),)),
    }


def attend(rows, allowed, live):
    length = rows.shape[0]
    split = rows.reshape(length, 3, HEADS, HSIZE).astype(jnp.float32)
    queries = split[:, 0]
    keys = split[:, 1]
    values = split[:, 2]
    scores = jnp.einsum('qhd,khd->hqk', queries, keys) * HSIZE ** (-0.5)
    scores = jnp.where(allowed[None], scores, -1000000000.0)
    probs = jax.nn.softmax(scores, axis=-1).astype(jnp.bfloat16)
    mixed = jnp.einsum('hqk,khd->qhd', probs.astype(jnp.float32), values)
    mixed = jnp.where(live[:, None, None], mixed, 0.0)
    return mixed.reshape(length, HEADS * HSIZE).astype(jnp.bfloat16)

def clip_start(counts, which):
    starts = jnp.cumsum(counts) - counts
    clips = jnp.arange(counts.shape[0], dtype=jnp.int32)
    return (jnp.sum(jnp.where(clips == which, starts, 0)), jnp.sum(jnp.where(clips == which, counts, 0)))

def home_masks(counts, moving, rank):
    ends = jnp.cumsum(counts)
    places = jnp.arange(TOK_DEV, dtype=jnp.int32)
    segment = lax.optimization_barrier(jnp.sum((places[:, None] >= ends[None, :]).astype(jnp.int32), axis=1))
    clips = jnp.arange(counts.shape[0], dtype=jnp.int32)
    gone = jnp.any((moving[:, 0:1] == rank) & (moving[:, 2:3] == clips[None, :]), axis=0)
    stays = jnp.logical_not(jnp.any((segment[:, None] == clips[None, :]) & gone[None, :], axis=1))
    return (segment[:, None] == segment[None, :], stays)

def reference(qkv, grad_out, lengths, moves, out_weight):

    def column(total, index):
        rows = qkv[:, index]
        cotan = grad_out[:, index]
        counts_all = lengths[:, index]
        moving = moves[index]
        padded = jnp.concatenate([rows, jnp.zeros((N_DP, CLIP_MAX, 3, HD), rows.dtype)], axis=1)
        cot_pad = jnp.concatenate([cotan, jnp.zeros((N_DP, CLIP_MAX, DOUT), cotan.dtype)], axis=1)
        box_list = []
        for step in range(MOVES):
            source = moving[step, 0]
            offset, length = clip_start(counts_all[source], moving[step, 2])
            piece_rows = lax.dynamic_slice_in_dim(padded[source], offset.astype(jnp.int32), CLIP_MAX, 0)
            piece_cot = lax.dynamic_slice_in_dim(cot_pad[source], offset.astype(jnp.int32), CLIP_MAX, 0)
            box_list.append((moving[step, 1], piece_rows, piece_cot, length))

        def device(rank, home_rows, home_cot, counts):
            allowed_home, stays = home_masks(counts, moving, rank)
            box_rows = jnp.zeros((CLIP_MAX, 3, HD), jnp.bfloat16)
            box_cot = jnp.zeros((CLIP_MAX, DOUT), jnp.bfloat16)
            box_len = jnp.zeros((), jnp.int32)
            for target, piece_rows, piece_cot, length in box_list:
                mine = target == rank
                box_rows = jnp.where(mine, piece_rows, box_rows)
                box_cot = jnp.where(mine, piece_cot, box_cot)
                box_len = jnp.where(mine, length.astype(jnp.int32), box_len)
            places = jnp.arange(CLIP_MAX, dtype=jnp.int32)
            box_live = places < box_len
            box_allowed = jnp.broadcast_to(box_live[None, :], (CLIP_MAX, CLIP_MAX))

            def forward(home_in, box_in):
                return (attend(home_in, allowed_home, stays), attend(box_in, box_allowed, box_live))
            (mixed_home, mixed_box), pullback = jax.vjp(forward, home_rows, box_rows)
            mixed_all = jnp.concatenate([mixed_home, mixed_box], axis=0)
            cot_all = jnp.concatenate([home_cot, box_cot], axis=0)
            back = lax.dot_general(cot_all, out_weight, (((1,), (1,)), ((), ())), preferred_element_type=jnp.float32).astype(jnp.bfloat16)
            grad_home, grad_box = pullback((back[:TOK_DEV], back[TOK_DEV:]))
            term = lax.dot_general(mixed_all, cot_all, (((0,), (0,)), ((), ())), preferred_element_type=jnp.float32)
            term = lax.optimization_barrier(term.astype(jnp.bfloat16))
            return (grad_home, grad_box, term)
        grad_home, grad_box, terms = jax.vmap(device)(jnp.arange(N_DP, dtype=jnp.int32), rows, cotan, counts_all)
        return (total + lax.optimization_barrier(jnp.sum(terms.astype(jnp.float32), axis=0)), (grad_home, grad_box))
    start = jnp.zeros((HD, DOUT), jnp.float32)
    weight_grad, stacked = lax.scan(column, start, jnp.arange(N_FSDP, dtype=jnp.int32))
    home_grad = jnp.swapaxes(stacked[0], 0, 1)
    inbox_grad = jnp.swapaxes(stacked[1], 0, 1)
    return (home_grad, inbox_grad, weight_grad)
```

```python
import jax
import jax.numpy as jnp
from jax import lax
from jax.experimental import pallas as pl
from jax.experimental.pallas import tpu as pltpu
from jax.sharding import PartitionSpec as P

HEADS = 8
HSIZE = 112
TOK_DEV = 192
CLIP_MAX = 128


def passed_along(shard, axis, by):
    length = lax.axis_size(axis)
    return lax.ppermute(shard, axis, [(i, (i + by) % length) for i in range(length)])


def attend(rows, allowed, live):
    length = rows.shape[0]
    split = rows.reshape(length, 3, HEADS, HSIZE)
    queries = split[:, 0]
    keys = split[:, 1]
    values = split[:, 2]
    scores = jnp.einsum(
        "qhd,khd->hqk", queries, keys, preferred_element_type=jnp.float32
    ) * HSIZE ** (-0.5)
    scores = jnp.where(allowed[None], scores, -1000000000.0)
    probs = jax.nn.softmax(scores, axis=-1).astype(jnp.bfloat16)
    mixed = jnp.einsum("hqk,khd->qhd", probs, values, preferred_element_type=jnp.float32)
    mixed = jnp.where(live[:, None, None], mixed, 0.0)
    return mixed.reshape(length, HEADS * HSIZE).astype(jnp.bfloat16)


def clip_start(counts, which):
    starts = jnp.cumsum(counts) - counts
    clips = jnp.arange(counts.shape[0], dtype=jnp.int32)
    return (
        jnp.sum(jnp.where(clips == which, starts, 0)),
        jnp.sum(jnp.where(clips == which, counts, 0)),
    )


def home_masks(counts, moving, rank):
    ends = jnp.cumsum(counts)
    places = jnp.arange(TOK_DEV, dtype=jnp.int32)
    segment = jnp.sum((places[:, None] >= ends[None, :]).astype(jnp.int32), axis=1)
    clips = jnp.arange(counts.shape[0], dtype=jnp.int32)
    gone = jnp.any((moving[:, 0:1] == rank) & (moving[:, 2:3] == clips[None, :]), axis=0)
    stays = jnp.logical_not(jnp.any((segment[:, None] == clips[None, :]) & gone[None, :], axis=1))
    return (segment[:, None] == segment[None, :], stays)


def local(qkv, grad_out, lengths, moves, out_weight):
    home_rows = qkv[0, 0]
    home_cot = grad_out[0, 0]
    counts_all = lengths[:, 0]
    moving = moves[0]
    rank = lax.axis_index("dp")
    ranks = jnp.arange(counts_all.shape[0], dtype=jnp.int32)
    counts = jnp.sum(jnp.where((ranks == rank)[:, None], counts_all, 0), axis=0)
    allowed_home, stays = home_masks(counts, moving, rank)
    padded = jnp.concatenate(
        [home_rows, jnp.zeros((CLIP_MAX,) + home_rows.shape[1:], home_rows.dtype)], axis=0
    )
    cot_pad = jnp.concatenate(
        [home_cot, jnp.zeros((CLIP_MAX, home_cot.shape[1]), home_cot.dtype)], axis=0
    )
    send_off = jnp.zeros((), jnp.int32)
    sending = jnp.zeros((), jnp.bool_)
    box_len = jnp.zeros((), jnp.int32)
    receiving = jnp.zeros((), jnp.bool_)
    for step in range(moving.shape[0]):
        source = moving[step, 0]
        which = moving[step, 2]
        mine_out = source == rank
        offset, unused = clip_start(counts, which)
        send_off = jnp.where(mine_out, offset, send_off)
        sending = jnp.logical_or(sending, mine_out)
        source_counts = jnp.sum(jnp.where((ranks == source)[:, None], counts_all, 0), axis=0)
        ignored, length = clip_start(source_counts, which)
        mine_in = moving[step, 1] == rank
        box_len = jnp.where(mine_in, length, box_len)
        receiving = jnp.logical_or(receiving, mine_in)
    out_rows = jnp.where(
        sending,
        lax.dynamic_slice_in_dim(padded, send_off, CLIP_MAX, 0),
        jnp.zeros((), jnp.bfloat16),
    )
    out_cot = jnp.where(
        sending,
        lax.dynamic_slice_in_dim(cot_pad, send_off, CLIP_MAX, 0),
        jnp.zeros((), jnp.bfloat16),
    )
    got_rows, got_cot = passed_along((out_rows, out_cot), "dp", 1)
    box_rows = jnp.where(receiving, got_rows, jnp.zeros((), jnp.bfloat16))
    box_cot = jnp.where(receiving, got_cot, jnp.zeros((), jnp.bfloat16))
    places = jnp.arange(CLIP_MAX, dtype=jnp.int32)
    box_live = places < box_len
    box_allowed = jnp.broadcast_to(box_live[None, :], (CLIP_MAX, CLIP_MAX))

    def forward(home_in, box_in):
        return (attend(home_in, allowed_home, stays), attend(box_in, box_allowed, box_live))

    (mixed_home, mixed_box), pullback = jax.vjp(forward, home_rows, box_rows)
    weights = lax.all_gather(out_weight, "fsdp", axis=0, tiled=True)
    mixed_all = jnp.concatenate([mixed_home, mixed_box], axis=0)
    cot_all = jnp.concatenate([home_cot, box_cot], axis=0)
    back = lax.dot_general(
        cot_all, weights, (((1,), (1,)), ((), ())), preferred_element_type=jnp.float32
    ).astype(jnp.bfloat16)
    tokens_dev = home_rows.shape[0]
    grad_home, grad_box = pullback((back[:tokens_dev], back[tokens_dev:]))
    shard_rows = out_weight.shape[0]
    rank_sum = lax.psum_scatter(
        lax.dot_general(
            cot_all, mixed_all, (((0,), (0,)), ((), ())), preferred_element_type=jnp.float32
        ).astype(jnp.bfloat16),
        "dp",
        scatter_dimension=0,
        tiled=True,
    ).astype(jnp.float32)
    whole = lax.psum(rank_sum, "fsdp")
    piece = lax.dynamic_slice_in_dim(whole, lax.axis_index("fsdp") * shard_rows, shard_rows, 1)
    weight_grad = jnp.transpose(piece)
    return (grad_home[None, None], grad_box[None, None], weight_grad)


F32 = jnp.float32
BF16 = jnp.bfloat16
CUT = 64


def dot(a, b, dims):
    return lax.dot_general(a, b, ((dims[:1], dims[1:]), ((), ())), preferred_element_type=F32)


def block_kernel(
    lens_ref, moves_ref, qkv_ref, g_ref, w_ref,
    home_ref, box_ref, wg_ref,
    w_all, probs, backs, t_own, t_core, chip, x_first, y_first, x_mid, y_mid, x_last, y_last,
    z_out, z_in, box_out,
    w_send, w_recv, c_send, c_recv, r_send, r_recv, z_send, z_recv, b_send, b_recv,
):
    rank, col = lax.axis_index("dp"), lax.axis_index("fsdp")
    core = lax.rem(col, 2)
    px = lax.rem(col // 2, 2)
    py = col // 4
    other_core = col + 1 - 2 * core
    other_x = col + 2 - 4 * px
    other_y = col + 4 - 8 * py
    diagonal = other_x + 4 - 8 * py
    n_dp = lax.axis_size("dp")
    pad = HSIZE

    def to_col(target):
        return {"dp": rank, "fsdp": target}

    def to_rank(target):
        return {"dp": target, "fsdp": col}

    def push(src, dst, send, recv, target):
        copy = pltpu.make_async_remote_copy(
            src_ref=src, dst_ref=dst, send_sem=send, recv_sem=recv,
            device_id=target, device_id_type=pl.DeviceIdType.MESH,
        )
        copy.start()
        return copy

    barrier = pltpu.get_barrier_semaphore()
    partners = [to_col(other_core), to_col(other_x), to_col(other_y)]
    partners += [to_rank(lax.rem(rank + k, n_dp)) for k in range(1, n_dp)]
    for partner in partners:
        pl.semaphore_signal(barrier, inc=1, device_id=partner, device_id_type=pl.DeviceIdType.MESH)
    pl.semaphore_wait(barrier, len(partners))

    def w_rows(owner, begin=0, count=pad):
        return w_all.at[pl.ds(pl.multiple_of(owner * pad + begin, 16), count)]

    def w_push(slot, src, owner, target, begin=0, count=pad):
        return push(src, w_rows(owner, begin, count), w_send.at[slot], w_recv.at[slot], to_col(target))

    started = []
    w_x = w_push(0, w_ref, col, other_x)
    w_y = w_push(1, w_ref, col, other_y)
    w_c = w_push(2, w_ref, col, other_core)
    started += [w_x, w_y, w_c]
    w_all[pl.ds(pl.multiple_of(col * pad, 16), pad)] = w_ref[...]

    l0, l1, l2 = lens_ref[rank, 0], lens_ref[rank, 1], lens_ref[rank, 2]
    e0, e1 = l0, l0 + l1
    n_tok = g_ref.shape[0]

    def seg_of(places):
        return (places >= e0).astype(jnp.int32) + (places >= e1).astype(jnp.int32)

    allowed = seg_of(lax.broadcasted_iota(jnp.int32, (n_tok, n_tok), 0)) == seg_of(
        lax.broadcasted_iota(jnp.int32, (n_tok, n_tok), 1))
    gone = []
    for clip in range(3):
        flag = jnp.int32(0)
        for m in range(moves_ref.shape[0]):
            hit = jnp.logical_and(moves_ref[m, 0] == rank, moves_ref[m, 2] == clip)
            flag = jnp.where(hit, jnp.int32(1), flag)
        gone.append(flag)
    start, count = jnp.int32(0), jnp.int32(0)
    for m in range(moves_ref.shape[0]):
        mine, which = moves_ref[m, 0] == rank, moves_ref[m, 2]
        begin = jnp.where(which == 0, jnp.int32(0), jnp.where(which == 1, e0, e1))
        length = jnp.where(which == 0, l0, jnp.where(which == 1, l1, l2))
        start = jnp.where(mine, begin, start)
        count = jnp.where(mine, length, count)
    seg_row = seg_of(lax.broadcasted_iota(jnp.int32, (1, n_tok), 1))
    gone_row = jnp.where(seg_row == 0, gone[0], jnp.where(seg_row == 1, gone[1], gone[2]))
    stay_row = (1 - gone_row).astype(F32)
    pick_t = lax.broadcasted_iota(jnp.int32, (n_tok, CLIP_MAX), 0)
    pick_i = lax.broadcasted_iota(jnp.int32, (n_tok, CLIP_MAX), 1)
    picked = jnp.logical_and(pick_t == pick_i + start, pick_i < count)
    pick = jnp.where(picked, jnp.float32(1), jnp.float32(0)).astype(BF16)

    cot = g_ref[...]
    c_copies = []
    for h in range(HEADS):
        rows = pl.ds(h * pad, pad)
        q, k, v = qkv_ref[0, rows], qkv_ref[1, rows], qkv_ref[2, rows]
        scores = dot(k, q, (0, 0)) * HSIZE ** (-0.5)
        scores = jnp.where(allowed, scores, -1000000000.0)
        top = jnp.max(scores, axis=0, keepdims=True)
        e = jnp.exp(scores - top)
        p = (e * (1.0 / jnp.sum(e, axis=0, keepdims=True))).astype(BF16)
        probs[h] = p
        mixed = dot(v, p, (1, 0)).astype(BF16)
        t_own[h % 2, h // 2] = dot(mixed, cot, (1, 0)).astype(BF16)
        if h % 2 == 1:
            m = h // 2
            c_copies.append(push(t_own.at[1 - core, m], t_core.at[m], c_send.at[m], c_recv.at[m], to_col(other_core)))
        if h == 3:
            w_x.wait_recv()
            diag_a = w_push(3, w_rows(other_x, 0, CUT), other_x, other_y, 0, CUT)
            pass_x = w_push(5, w_rows(other_x), other_x, other_core)
            w_y.wait_recv()
            diag_b = w_push(4, w_rows(other_y, CUT, pad - CUT), other_y, other_x, CUT, pad - CUT)
            pass_y = w_push(6, w_rows(other_y), other_y, other_core)
            started += [diag_a, pass_x, diag_b, pass_y]
    started += c_copies

    def r_push(slot, src, dst, target):
        copy = push(src, dst, r_send.at[slot], r_recv.at[slot], to_col(target))
        started.append(copy)
        return copy

    low, high = pl.ds(0, CUT), pl.ds(CUT, pad - CUT)
    for m in range(4):
        c_copies[m].wait_recv()
        chip[m] = (t_own[core, m].astype(F32) + t_core[m].astype(F32)).astype(BF16)
    to_x = [r_push(i, chip.at[2 * i + 1 - px, low], x_first.at[i], other_x) for i in range(2)]
    to_y = [r_push(2 + i, chip.at[2 * (1 - py) + i, high], y_first.at[i], other_y) for i in range(2)]

    diag_a.wait_recv()
    pass_a = w_push(7, w_rows(diagonal, 0, CUT), diagonal, other_core, 0, CUT)
    diag_b.wait_recv()
    pass_b = w_push(8, w_rows(diagonal, CUT, pad - CUT), diagonal, other_core, CUT, pad - CUT)
    started += [pass_a, pass_b]
    for copy in (w_c, pass_x, pass_y, pass_a, pass_b):
        copy.wait_recv()
    backs[...] = dot(w_all[...], cot, (1, 1)).astype(BF16)

    boxes = []
    for h in range(HEADS):
        rows = pl.ds(h * pad, pad)
        q, k, v = qkv_ref[0, rows], qkv_ref[1, rows], qkv_ref[2, rows]
        p, back = probs[h], backs[rows]
        dp = dot(v, back, (0, 0))
        pf = p.astype(F32)
        ds = pf * (dp - jnp.sum(pf * dp, axis=0, keepdims=True))
        ds = (ds * HSIZE ** (-0.5)).astype(BF16)
        grads = (dot(k, ds, (1, 0)), dot(q, ds, (1, 1)), dot(back, p, (1, 1)))
        for i, grad in enumerate(grads):
            home_ref[i, rows] = (grad * stay_row).astype(BF16)
            box_out[h, i] = dot(grad.astype(BF16), pick, (1, 0)).astype(BF16)
        boxes.append(push(box_out.at[h], box_ref.at[h], b_send.at[h], b_recv.at[h], to_rank(lax.rem(rank + 1, n_dp))))
        if h == 2:
            for i in range(2):
                to_x[i].wait_recv()
                x_mid[i] = (chip[2 * i + px, low].astype(F32) + x_first[i].astype(F32)).astype(BF16)
                to_y[i].wait_recv()
                y_mid[i] = (chip[2 * py + i, high].astype(F32) + y_first[i].astype(F32)).astype(BF16)
            then_y = r_push(4, x_mid.at[1 - py], y_last, other_y)
            then_x = r_push(5, y_mid.at[1 - px], x_last, other_x)
        if h == 5:
            then_y.wait_recv()
            then_x.wait_recv()
            own_low = x_mid[py].astype(F32) + y_last[...].astype(F32)
            own_high = y_mid[px].astype(F32) + x_last[...].astype(F32)
            width = z_out.shape[2]
            for part in range(n_dp):
                cut = slice(part * width, (part + 1) * width)
                z_out[part, low] = own_low[:, cut].astype(BF16)
                z_out[part, high] = own_high[:, cut].astype(BF16)
            z_copies = []
            for step in range(1, n_dp):
                target = lax.rem(rank + step, n_dp)
                z_copies.append(push(z_out.at[target], z_in.at[step - 1], z_send.at[step - 1], z_recv.at[step - 1], to_rank(target)))
    started += boxes + z_copies
    total = z_out[rank].astype(F32)
    for step, copy in enumerate(z_copies):
        copy.wait_recv()
        total += z_in[step].astype(F32)
    wg_ref[...] = total
    for copy in boxes:
        copy.wait_recv()
    for copy in started:
        copy.wait_send()


def fused(qkv, grad_out, lengths, moves, out_weight):
    n_dp = lax.axis_size("dp")
    tok, feats = qkv.shape[2], qkv.shape[4]
    dout = grad_out.shape[3]
    pad, rest, width = HSIZE, HSIZE - CUT, dout // n_dp
    vmem = pl.BlockSpec(memory_space=pltpu.VMEM)
    smem = pl.BlockSpec(memory_space=pltpu.SMEM)
    features = jnp.transpose(qkv[0, 0], (1, 2, 0))
    home, box, weight_grad = pl.pallas_call(
        block_kernel,
        out_shape=(
            jax.ShapeDtypeStruct((3, feats, tok), BF16),
            jax.ShapeDtypeStruct((HEADS, 3, pad, CLIP_MAX), BF16),
            jax.ShapeDtypeStruct((pad, width), F32),
        ),
        in_specs=[smem, smem, vmem, vmem, vmem],
        out_specs=(vmem, vmem, vmem),
        scratch_shapes=[
            pltpu.VMEM((feats, dout), BF16),
            pltpu.VMEM((HEADS, tok, tok), BF16),
            pltpu.VMEM((feats, tok), BF16),
            pltpu.VMEM((2, 4, pad, dout), BF16),
            pltpu.VMEM((4, pad, dout), BF16),
            pltpu.VMEM((4, pad, dout), BF16),
            pltpu.VMEM((2, CUT, dout), BF16),
            pltpu.VMEM((2, rest, dout), BF16),
            pltpu.VMEM((2, CUT, dout), BF16),
            pltpu.VMEM((2, rest, dout), BF16),
            pltpu.VMEM((rest, dout), BF16),
            pltpu.VMEM((CUT, dout), BF16),
            pltpu.VMEM((n_dp, pad, width), BF16),
            pltpu.VMEM((n_dp - 1, pad, width), BF16),
            pltpu.VMEM((HEADS, 3, pad, CLIP_MAX), BF16),
        ] + [pltpu.SemaphoreType.DMA((n,)) for n in (9, 9, 4, 4, 6, 6, n_dp - 1, n_dp - 1, HEADS, HEADS)],
        compiler_params=pltpu.CompilerParams(
            collective_id=0, has_side_effects=True, vmem_limit_bytes=40 * 1024 * 1024
        ),
        name="block",
    )(lengths[:, 0], moves[0], features, grad_out[0, 0], out_weight)
    home_grad = jnp.transpose(home, (2, 0, 1))
    inbox_grad = jnp.transpose(box, (3, 1, 0, 2)).reshape(CLIP_MAX, 3, feats)
    return (home_grad[None, None], inbox_grad[None, None], weight_grad)


def solution(mesh):
    small = mesh.shape["dp"] == 4 and mesh.shape["fsdp"] == 8
    placed = (
        P("dp", "fsdp", None, None, None),
        P("dp", "fsdp", None, None),
        P(None, "fsdp", None),
        P("fsdp", None, None),
        P("fsdp", None),
    )
    return jax.shard_map(
        fused if small else local,
        mesh=mesh,
        in_specs=placed,
        out_specs=(
            P("dp", "fsdp", None, None, None),
            P("dp", "fsdp", None, None, None),
            P("fsdp", "dp"),
        ),
        check_vma=False,
    )
```

```python
import jax
import jax.numpy as jnp
from jax import lax
from jax.experimental import pallas as pl
from jax.experimental.pallas import tpu as pltpu
from jax.sharding import PartitionSpec as P

HEADS = 8
HSIZE = 112
TOK_DEV = 192
CLIP_MAX = 128


def passed_along(shard, axis, by):
    length = lax.axis_size(axis)
    return lax.ppermute(shard, axis, [(i, (i + by) % length) for i in range(length)])


def attend(rows, allowed, live):
    length = rows.shape[0]
    split = rows.reshape(length, 3, HEADS, HSIZE)
    queries = split[:, 0]
    keys = split[:, 1]
    values = split[:, 2]
    scores = jnp.einsum(
        "qhd,khd->hqk", queries, keys, preferred_element_type=jnp.float32
    ) * HSIZE ** (-0.5)
    scores = jnp.where(allowed[None], scores, -1000000000.0)
    probs = jax.nn.softmax(scores, axis=-1).astype(jnp.bfloat16)
    mixed = jnp.einsum("hqk,khd->qhd", probs, values, preferred_element_type=jnp.float32)
    mixed = jnp.where(live[:, None, None], mixed, 0.0)
    return mixed.reshape(length, HEADS * HSIZE).astype(jnp.bfloat16)


def clip_start(counts, which):
    starts = jnp.cumsum(counts) - counts
    clips = jnp.arange(counts.shape[0], dtype=jnp.int32)
    return (
        jnp.sum(jnp.where(clips == which, starts, 0)),
        jnp.sum(jnp.where(clips == which, counts, 0)),
    )


def home_masks(counts, moving, rank):
    ends = jnp.cumsum(counts)
    places = jnp.arange(TOK_DEV, dtype=jnp.int32)
    segment = jnp.sum((places[:, None] >= ends[None, :]).astype(jnp.int32), axis=1)
    clips = jnp.arange(counts.shape[0], dtype=jnp.int32)
    gone = jnp.any((moving[:, 0:1] == rank) & (moving[:, 2:3] == clips[None, :]), axis=0)
    stays = jnp.logical_not(jnp.any((segment[:, None] == clips[None, :]) & gone[None, :], axis=1))
    return (segment[:, None] == segment[None, :], stays)


def local(qkv, grad_out, lengths, moves, out_weight):
    home_rows = qkv[0, 0]
    home_cot = grad_out[0, 0]
    counts_all = lengths[:, 0]
    moving = moves[0]
    rank = lax.axis_index("dp")
    ranks = jnp.arange(counts_all.shape[0], dtype=jnp.int32)
    counts = jnp.sum(jnp.where((ranks == rank)[:, None], counts_all, 0), axis=0)
    allowed_home, stays = home_masks(counts, moving, rank)
    padded = jnp.concatenate(
        [home_rows, jnp.zeros((CLIP_MAX,) + home_rows.shape[1:], home_rows.dtype)], axis=0
    )
    cot_pad = jnp.concatenate(
        [home_cot, jnp.zeros((CLIP_MAX, home_cot.shape[1]), home_cot.dtype)], axis=0
    )
    send_off = jnp.zeros((), jnp.int32)
    sending = jnp.zeros((), jnp.bool_)
    box_len = jnp.zeros((), jnp.int32)
    receiving = jnp.zeros((), jnp.bool_)
    for step in range(moving.shape[0]):
        source = moving[step, 0]
        which = moving[step, 2]
        mine_out = source == rank
        offset, unused = clip_start(counts, which)
        send_off = jnp.where(mine_out, offset, send_off)
        sending = jnp.logical_or(sending, mine_out)
        source_counts = jnp.sum(jnp.where((ranks == source)[:, None], counts_all, 0), axis=0)
        ignored, length = clip_start(source_counts, which)
        mine_in = moving[step, 1] == rank
        box_len = jnp.where(mine_in, length, box_len)
        receiving = jnp.logical_or(receiving, mine_in)
    out_rows = jnp.where(
        sending,
        lax.dynamic_slice_in_dim(padded, send_off, CLIP_MAX, 0),
        jnp.zeros((), jnp.bfloat16),
    )
    out_cot = jnp.where(
        sending,
        lax.dynamic_slice_in_dim(cot_pad, send_off, CLIP_MAX, 0),
        jnp.zeros((), jnp.bfloat16),
    )
    got_rows, got_cot = passed_along((out_rows, out_cot), "dp", 1)
    box_rows = jnp.where(receiving, got_rows, jnp.zeros((), jnp.bfloat16))
    box_cot = jnp.where(receiving, got_cot, jnp.zeros((), jnp.bfloat16))
    places = jnp.arange(CLIP_MAX, dtype=jnp.int32)
    box_live = places < box_len
    box_allowed = jnp.broadcast_to(box_live[None, :], (CLIP_MAX, CLIP_MAX))

    def forward(home_in, box_in):
        return (attend(home_in, allowed_home, stays), attend(box_in, box_allowed, box_live))

    (mixed_home, mixed_box), pullback = jax.vjp(forward, home_rows, box_rows)
    weights = lax.all_gather(out_weight, "fsdp", axis=0, tiled=True)
    mixed_all = jnp.concatenate([mixed_home, mixed_box], axis=0)
    cot_all = jnp.concatenate([home_cot, box_cot], axis=0)
    back = lax.dot_general(
        cot_all, weights, (((1,), (1,)), ((), ())), preferred_element_type=jnp.float32
    ).astype(jnp.bfloat16)
    tokens_dev = home_rows.shape[0]
    grad_home, grad_box = pullback((back[:tokens_dev], back[tokens_dev:]))
    shard_rows = out_weight.shape[0]
    rank_sum = lax.psum_scatter(
        lax.dot_general(
            cot_all, mixed_all, (((0,), (0,)), ((), ())), preferred_element_type=jnp.float32
        ).astype(jnp.bfloat16),
        "dp",
        scatter_dimension=0,
        tiled=True,
    ).astype(jnp.float32)
    whole = lax.psum(rank_sum, "fsdp")
    piece = lax.dynamic_slice_in_dim(whole, lax.axis_index("fsdp") * shard_rows, shard_rows, 1)
    weight_grad = jnp.transpose(piece)
    return (grad_home[None, None], grad_box[None, None], weight_grad)


F32 = jnp.float32
BF16 = jnp.bfloat16
CUT = 64


def dot(a, b, dims):
    return lax.dot_general(a, b, ((dims[:1], dims[1:]), ((), ())), preferred_element_type=F32)


def block_kernel(
    lens_hbm, moves_hbm, qkv_hbm, g_hbm, w_ref,
    home_ref, box_ref, wg_ref,
    lens_ref, moves_ref, nat_ref, qkv_ref, g_ref, home_t, box_in, w_all, probs, backs, t_own, t_core, chip, x_first, y_first, x_mid, y_mid, x_last, y_last,
    z_out, z_in, box_out,
    in_sem, w_send, w_recv, c_send, c_recv, r_send, r_recv, z_send, z_recv, b_send, b_recv,
):
    rank, col = lax.axis_index("dp"), lax.axis_index("fsdp")
    core = lax.rem(col, 2)
    px = lax.rem(col // 2, 2)
    py = col // 4
    other_core = col + 1 - 2 * core
    other_x = col + 2 - 4 * px
    other_y = col + 4 - 8 * py
    diagonal = other_x + 4 - 8 * py
    n_dp = lax.axis_size("dp")
    pad = HSIZE

    def to_col(target):
        return {"dp": rank, "fsdp": target}

    def to_rank(target):
        return {"dp": target, "fsdp": col}

    def push(src, dst, send, recv, target):
        copy = pltpu.make_async_remote_copy(
            src_ref=src, dst_ref=dst, send_sem=send, recv_sem=recv,
            device_id=target, device_id_type=pl.DeviceIdType.MESH,
        )
        copy.start()
        return copy

    fetches = [
        pltpu.make_async_copy(src, dst, in_sem.at[i]) for i, (src, dst) in enumerate((
            (lens_hbm, lens_ref), (moves_hbm, moves_ref), (qkv_hbm.at[0], nat_ref.at[0]),
            (qkv_hbm.at[1], nat_ref.at[1]), (qkv_hbm.at[2], nat_ref.at[2]), (g_hbm, g_ref),
            (w_ref, w_all.at[pl.ds(pl.multiple_of(col * pad, 16), pad)])))
    ]
    for fetch in fetches:
        fetch.start()
    barrier = pltpu.get_barrier_semaphore()
    partners = [to_col(other_core), to_col(other_x), to_col(other_y)]
    partners += [to_rank(lax.rem(rank + k, n_dp)) for k in range(1, n_dp)]
    for partner in partners:
        pl.semaphore_signal(barrier, inc=1, device_id=partner, device_id_type=pl.DeviceIdType.MESH)
    pl.semaphore_wait(barrier, len(partners))

    def w_rows(owner, begin=0, count=pad):
        return w_all.at[pl.ds(pl.multiple_of(owner * pad + begin, 16), count)]

    def w_push(slot, src, owner, target, begin=0, count=pad):
        return push(src, w_rows(owner, begin, count), w_send.at[slot], w_recv.at[slot], to_col(target))

    started = []
    w_x = w_push(0, w_ref, col, other_x)
    w_y = w_push(1, w_ref, col, other_y)
    w_c = w_push(2, w_ref, col, other_core)
    started += [w_x, w_y, w_c]
    for fetch in fetches:
        fetch.wait()
    for i in range(3):
        qkv_ref[i] = nat_ref[i].T

    l0, l1, l2 = lens_ref[0, 0, rank], lens_ref[1, 0, rank], lens_ref[2, 0, rank]
    e0, e1 = l0, l0 + l1
    n_tok = g_ref.shape[0]

    def seg_of(places):
        return (places >= e0).astype(jnp.int32) + (places >= e1).astype(jnp.int32)

    allowed = seg_of(lax.broadcasted_iota(jnp.int32, (n_tok, n_tok), 0)) == seg_of(
        lax.broadcasted_iota(jnp.int32, (n_tok, n_tok), 1))
    gone = []
    for clip in range(3):
        flag = jnp.int32(0)
        for m in range(moves_ref.shape[1]):
            hit = jnp.logical_and(moves_ref[0, m, 0] == rank, moves_ref[0, m, 2] == clip)
            flag = jnp.where(hit, jnp.int32(1), flag)
        gone.append(flag)
    start, count = jnp.int32(0), jnp.int32(0)
    for m in range(moves_ref.shape[1]):
        mine, which = moves_ref[0, m, 0] == rank, moves_ref[0, m, 2]
        begin = jnp.where(which == 0, jnp.int32(0), jnp.where(which == 1, e0, e1))
        length = jnp.where(which == 0, l0, jnp.where(which == 1, l1, l2))
        start = jnp.where(mine, begin, start)
        count = jnp.where(mine, length, count)
    seg_row = seg_of(lax.broadcasted_iota(jnp.int32, (1, n_tok), 1))
    gone_row = jnp.where(seg_row == 0, gone[0], jnp.where(seg_row == 1, gone[1], gone[2]))
    stay_row = (1 - gone_row).astype(F32)
    pick_t = lax.broadcasted_iota(jnp.int32, (n_tok, CLIP_MAX), 0)
    pick_i = lax.broadcasted_iota(jnp.int32, (n_tok, CLIP_MAX), 1)
    picked = jnp.logical_and(pick_t == pick_i + start, pick_i < count)
    pick = jnp.where(picked, jnp.float32(1), jnp.float32(0)).astype(BF16)

    cot = g_ref[...]
    c_copies = []
    for h in range(HEADS):
        rows = pl.ds(h * pad, pad)
        q, k, v = qkv_ref[0, rows], nat_ref[1, :, h * pad:(h + 1) * pad], qkv_ref[2, rows]
        scores = dot(k, q, (1, 0)) * HSIZE ** (-0.5)
        scores = jnp.where(allowed, scores, -1000000000.0)
        top = jnp.max(scores, axis=0, keepdims=True)
        e = jnp.exp(scores - top)
        p = (e * (1.0 / jnp.sum(e, axis=0, keepdims=True))).astype(BF16)
        probs[h] = p
        mixed = dot(v, p, (1, 0)).astype(BF16)
        t_own[h % 2, h // 2] = dot(mixed, cot, (1, 0)).astype(BF16)
        if h % 2 == 1:
            m = h // 2
            c_copies.append(push(t_own.at[1 - core, m], t_core.at[m], c_send.at[m], c_recv.at[m], to_col(other_core)))
        if h == 3:
            w_x.wait_recv()
            diag_a = w_push(3, w_rows(other_x, 0, CUT), other_x, other_y, 0, CUT)
            pass_x = w_push(5, w_rows(other_x), other_x, other_core)
            w_y.wait_recv()
            diag_b = w_push(4, w_rows(other_y, CUT, pad - CUT), other_y, other_x, CUT, pad - CUT)
            pass_y = w_push(6, w_rows(other_y), other_y, other_core)
            started += [diag_a, pass_x, diag_b, pass_y]
    started += c_copies

    def r_push(slot, src, dst, target):
        copy = push(src, dst, r_send.at[slot], r_recv.at[slot], to_col(target))
        started.append(copy)
        return copy

    low, high = pl.ds(0, CUT), pl.ds(CUT, pad - CUT)
    for m in range(4):
        c_copies[m].wait_recv()
        chip[m] = (t_own[core, m].astype(F32) + t_core[m].astype(F32)).astype(BF16)
    to_x = [r_push(i, chip.at[2 * i + 1 - px, low], x_first.at[i], other_x) for i in range(2)]
    to_y = [r_push(2 + i, chip.at[2 * (1 - py) + i, high], y_first.at[i], other_y) for i in range(2)]

    diag_a.wait_recv()
    pass_a = w_push(7, w_rows(diagonal, 0, CUT), diagonal, other_core, 0, CUT)
    diag_b.wait_recv()
    pass_b = w_push(8, w_rows(diagonal, CUT, pad - CUT), diagonal, other_core, CUT, pad - CUT)
    started += [pass_a, pass_b]
    for copy in (w_c, pass_x, pass_y, pass_a, pass_b):
        copy.wait_recv()
    backs[...] = dot(w_all[...], cot, (1, 1)).astype(BF16)

    boxes = []
    for h in range(HEADS):
        rows = pl.ds(h * pad, pad)
        q, k, v = qkv_ref[0, rows], qkv_ref[1, rows], nat_ref[2, :, h * pad:(h + 1) * pad]
        p, back = probs[h], backs[rows]
        dp = dot(v, back, (1, 0))
        pf = p.astype(F32)
        ds = pf * (dp - jnp.sum(pf * dp, axis=0, keepdims=True))
        ds = (ds * HSIZE ** (-0.5)).astype(BF16)
        grads = (dot(k, ds, (1, 0)), dot(q, ds, (1, 1)), dot(back, p, (1, 1)))
        for i, grad in enumerate(grads):
            home_t[i, rows] = (grad * stay_row).astype(BF16)
            box_out[i, h] = dot(grad.astype(BF16), pick, (1, 0)).astype(BF16)
        boxes.append(push(box_out.at[:, h], box_in.at[:, h], b_send.at[h], b_recv.at[h], to_rank(lax.rem(rank + 1, n_dp))))
        if h == 2:
            for i in range(2):
                to_x[i].wait_recv()
                x_mid[i] = (chip[2 * i + px, low].astype(F32) + x_first[i].astype(F32)).astype(BF16)
                to_y[i].wait_recv()
                y_mid[i] = (chip[2 * py + i, high].astype(F32) + y_first[i].astype(F32)).astype(BF16)
            then_y = r_push(4, x_mid.at[1 - py], y_last, other_y)
            then_x = r_push(5, y_mid.at[1 - px], x_last, other_x)
        if h == 5:
            then_y.wait_recv()
            then_x.wait_recv()
            own_low = x_mid[py].astype(F32) + y_last[...].astype(F32)
            own_high = y_mid[px].astype(F32) + x_last[...].astype(F32)
            width = z_out.shape[2]
            for part in range(n_dp):
                cut = slice(part * width, (part + 1) * width)
                z_out[part, low] = own_low[:, cut].astype(BF16)
                z_out[part, high] = own_high[:, cut].astype(BF16)
            z_copies = []
            for step in range(1, n_dp):
                target = lax.rem(rank + step, n_dp)
                z_copies.append(push(z_out.at[target], z_in.at[step - 1], z_send.at[step - 1], z_recv.at[step - 1], to_rank(target)))
    started += boxes + z_copies
    for i in range(3):
        home_ref[i] = home_t[i].T
    total = z_out[rank].astype(F32)
    for step, copy in enumerate(z_copies):
        copy.wait_recv()
        total += z_in[step].astype(F32)
    wg_ref[...] = total
    for copy in boxes:
        copy.wait_recv()
    for i in range(3):
        box_ref[i] = box_in[i].reshape(HEADS * pad, CLIP_MAX).T
    for copy in started:
        copy.wait_send()


def fused(qkv, grad_out, lengths, moves, out_weight):
    n_dp = lax.axis_size("dp")
    tok, feats = qkv.shape[2], qkv.shape[4]
    dout = grad_out.shape[3]
    pad, rest, width = HSIZE, HSIZE - CUT, dout // n_dp
    vmem = pl.BlockSpec(memory_space=pltpu.VMEM)
    hbm = pl.BlockSpec(memory_space=pltpu.HBM)
    natural = jnp.transpose(qkv[0, 0], (1, 0, 2))
    by_clip = jnp.transpose(lengths, (2, 1, 0))
    home, box, weight_grad = pl.pallas_call(
        block_kernel,
        out_shape=(
            jax.ShapeDtypeStruct((3, tok, feats), BF16),
            jax.ShapeDtypeStruct((3, CLIP_MAX, feats), BF16),
            jax.ShapeDtypeStruct((pad, width), F32),
        ),
        in_specs=[hbm] * 5,
        out_specs=(vmem, vmem, vmem),
        scratch_shapes=[
            pltpu.SMEM(by_clip.shape, jnp.int32),
            pltpu.SMEM(moves.shape, jnp.int32),
            pltpu.VMEM((3, tok, feats), BF16),
            pltpu.VMEM((3, feats, tok), BF16),
            pltpu.VMEM((tok, dout), BF16),
            pltpu.VMEM((3, feats, tok), BF16),
            pltpu.VMEM((3, HEADS, pad, CLIP_MAX), BF16),
            pltpu.VMEM((feats, dout), BF16),
            pltpu.VMEM((HEADS, tok, tok), BF16),
            pltpu.VMEM((feats, tok), BF16),
            pltpu.VMEM((2, 4, pad, dout), BF16),
            pltpu.VMEM((4, pad, dout), BF16),
            pltpu.VMEM((4, pad, dout), BF16),
            pltpu.VMEM((2, CUT, dout), BF16),
            pltpu.VMEM((2, rest, dout), BF16),
            pltpu.VMEM((2, CUT, dout), BF16),
            pltpu.VMEM((2, rest, dout), BF16),
            pltpu.VMEM((rest, dout), BF16),
            pltpu.VMEM((CUT, dout), BF16),
            pltpu.VMEM((n_dp, pad, width), BF16),
            pltpu.VMEM((n_dp - 1, pad, width), BF16),
            pltpu.VMEM((3, HEADS, pad, CLIP_MAX), BF16),
        ] + [pltpu.SemaphoreType.DMA((n,)) for n in (7, 9, 9, 4, 4, 6, 6, n_dp - 1, n_dp - 1, HEADS, HEADS)],
        compiler_params=pltpu.CompilerParams(
            collective_id=0, has_side_effects=True, vmem_limit_bytes=60 * 1024 * 1024
        ),
        name="block",
    )(by_clip, moves, natural, grad_out[0, 0], out_weight)
    home_grad = jnp.transpose(home, (1, 0, 2))
    inbox_grad = jnp.transpose(box, (1, 0, 2))
    return (home_grad[None, None], inbox_grad[None, None], weight_grad)


def solution(mesh):
    small = mesh.shape["dp"] == 4 and mesh.shape["fsdp"] == 8
    placed = (
        P("dp", "fsdp", None, None, None),
        P("dp", "fsdp", None, None),
        P(None, "fsdp", None),
        P("fsdp", None, None),
        P("fsdp", None),
    )
    return jax.shard_map(
        fused if small else local,
        mesh=mesh,
        in_specs=placed,
        out_specs=(
            P("dp", "fsdp", None, None, None),
            P("dp", "fsdp", None, None, None),
            P("fsdp", "dp"),
        ),
        check_vma=False,
    )
```

```python
import jax
import jax.numpy as jnp
from jax import lax
from jax.experimental import pallas as pl
from jax.experimental.pallas import tpu as pltpu
from jax.sharding import PartitionSpec as P

HEADS = 8
HSIZE = 112
TOK_DEV = 192
CLIP_MAX = 128


def passed_along(shard, axis, by):
    length = lax.axis_size(axis)
    return lax.ppermute(shard, axis, [(i, (i + by) % length) for i in range(length)])


def attend(rows, allowed, live):
    length = rows.shape[0]
    split = rows.reshape(length, 3, HEADS, HSIZE)
    queries = split[:, 0]
    keys = split[:, 1]
    values = split[:, 2]
    scores = jnp.einsum(
        "qhd,khd->hqk", queries, keys, preferred_element_type=jnp.float32
    ) * HSIZE ** (-0.5)
    scores = jnp.where(allowed[None], scores, -1000000000.0)
    probs = jax.nn.softmax(scores, axis=-1).astype(jnp.bfloat16)
    mixed = jnp.einsum("hqk,khd->qhd", probs, values, preferred_element_type=jnp.float32)
    mixed = jnp.where(live[:, None, None], mixed, 0.0)
    return mixed.reshape(length, HEADS * HSIZE).astype(jnp.bfloat16)


def clip_start(counts, which):
    starts = jnp.cumsum(counts) - counts
    clips = jnp.arange(counts.shape[0], dtype=jnp.int32)
    return (
        jnp.sum(jnp.where(clips == which, starts, 0)),
        jnp.sum(jnp.where(clips == which, counts, 0)),
    )


def home_masks(counts, moving, rank):
    ends = jnp.cumsum(counts)
    places = jnp.arange(TOK_DEV, dtype=jnp.int32)
    segment = jnp.sum((places[:, None] >= ends[None, :]).astype(jnp.int32), axis=1)
    clips = jnp.arange(counts.shape[0], dtype=jnp.int32)
    gone = jnp.any((moving[:, 0:1] == rank) & (moving[:, 2:3] == clips[None, :]), axis=0)
    stays = jnp.logical_not(jnp.any((segment[:, None] == clips[None, :]) & gone[None, :], axis=1))
    return (segment[:, None] == segment[None, :], stays)


def local(qkv, grad_out, lengths, moves, out_weight):
    home_rows = qkv[0, 0]
    home_cot = grad_out[0, 0]
    counts_all = lengths[:, 0]
    moving = moves[0]
    rank = lax.axis_index("dp")
    ranks = jnp.arange(counts_all.shape[0], dtype=jnp.int32)
    counts = jnp.sum(jnp.where((ranks == rank)[:, None], counts_all, 0), axis=0)
    allowed_home, stays = home_masks(counts, moving, rank)
    padded = jnp.concatenate(
        [home_rows, jnp.zeros((CLIP_MAX,) + home_rows.shape[1:], home_rows.dtype)], axis=0
    )
    cot_pad = jnp.concatenate(
        [home_cot, jnp.zeros((CLIP_MAX, home_cot.shape[1]), home_cot.dtype)], axis=0
    )
    send_off = jnp.zeros((), jnp.int32)
    sending = jnp.zeros((), jnp.bool_)
    box_len = jnp.zeros((), jnp.int32)
    receiving = jnp.zeros((), jnp.bool_)
    for step in range(moving.shape[0]):
        source = moving[step, 0]
        which = moving[step, 2]
        mine_out = source == rank
        offset, unused = clip_start(counts, which)
        send_off = jnp.where(mine_out, offset, send_off)
        sending = jnp.logical_or(sending, mine_out)
        source_counts = jnp.sum(jnp.where((ranks == source)[:, None], counts_all, 0), axis=0)
        ignored, length = clip_start(source_counts, which)
        mine_in = moving[step, 1] == rank
        box_len = jnp.where(mine_in, length, box_len)
        receiving = jnp.logical_or(receiving, mine_in)
    out_rows = jnp.where(
        sending,
        lax.dynamic_slice_in_dim(padded, send_off, CLIP_MAX, 0),
        jnp.zeros((), jnp.bfloat16),
    )
    out_cot = jnp.where(
        sending,
        lax.dynamic_slice_in_dim(cot_pad, send_off, CLIP_MAX, 0),
        jnp.zeros((), jnp.bfloat16),
    )
    got_rows, got_cot = passed_along((out_rows, out_cot), "dp", 1)
    box_rows = jnp.where(receiving, got_rows, jnp.zeros((), jnp.bfloat16))
    box_cot = jnp.where(receiving, got_cot, jnp.zeros((), jnp.bfloat16))
    places = jnp.arange(CLIP_MAX, dtype=jnp.int32)
    box_live = places < box_len
    box_allowed = jnp.broadcast_to(box_live[None, :], (CLIP_MAX, CLIP_MAX))

    def forward(home_in, box_in):
        return (attend(home_in, allowed_home, stays), attend(box_in, box_allowed, box_live))

    (mixed_home, mixed_box), pullback = jax.vjp(forward, home_rows, box_rows)
    weights = lax.all_gather(out_weight, "fsdp", axis=0, tiled=True)
    mixed_all = jnp.concatenate([mixed_home, mixed_box], axis=0)
    cot_all = jnp.concatenate([home_cot, box_cot], axis=0)
    back = lax.dot_general(
        cot_all, weights, (((1,), (1,)), ((), ())), preferred_element_type=jnp.float32
    ).astype(jnp.bfloat16)
    tokens_dev = home_rows.shape[0]
    grad_home, grad_box = pullback((back[:tokens_dev], back[tokens_dev:]))
    shard_rows = out_weight.shape[0]
    rank_sum = lax.psum_scatter(
        lax.dot_general(
            cot_all, mixed_all, (((0,), (0,)), ((), ())), preferred_element_type=jnp.float32
        ).astype(jnp.bfloat16),
        "dp",
        scatter_dimension=0,
        tiled=True,
    ).astype(jnp.float32)
    whole = lax.psum(rank_sum, "fsdp")
    piece = lax.dynamic_slice_in_dim(whole, lax.axis_index("fsdp") * shard_rows, shard_rows, 1)
    weight_grad = jnp.transpose(piece)
    return (grad_home[None, None], grad_box[None, None], weight_grad)


F32 = jnp.float32
BF16 = jnp.bfloat16
EARLY = 5
CUT = 64


def dot(a, b, dims):
    return lax.dot_general(a, b, ((dims[:1], dims[1:]), ((), ())), preferred_element_type=F32)


def block_kernel(
    lens_hbm, moves_hbm, qkv_hbm, g_hbm, w_ref,
    home_ref, box_ref, wg_ref,
    lens_ref, moves_ref, nat_ref, qkv_ref, g_ref, home_t, box_in, early_out, early_in, back_out, back_in, box_probs, w_all, probs, backs, t_own, t_core, chip, x_first, y_first, x_mid, y_mid, x_last, y_last,
    z_out, z_in, box_out,
    in_sem, w_send, w_recv, c_send, c_recv, r_send, r_recv, z_send, z_recv, b_send, b_recv, e_send, e_recv,
):
    rank, col = lax.axis_index("dp"), lax.axis_index("fsdp")
    core = lax.rem(col, 2)
    px = lax.rem(col // 2, 2)
    py = col // 4
    other_core = col + 1 - 2 * core
    other_x = col + 2 - 4 * px
    other_y = col + 4 - 8 * py
    diagonal = other_x + 4 - 8 * py
    n_dp = lax.axis_size("dp")
    pad = HSIZE

    def to_col(target):
        return {"dp": rank, "fsdp": target}

    def to_rank(target):
        return {"dp": target, "fsdp": col}

    def push(src, dst, send, recv, target):
        copy = pltpu.make_async_remote_copy(
            src_ref=src, dst_ref=dst, send_sem=send, recv_sem=recv,
            device_id=target, device_id_type=pl.DeviceIdType.MESH,
        )
        copy.start()
        return copy

    fetches = [
        pltpu.make_async_copy(src, dst, in_sem.at[i]) for i, (src, dst) in enumerate((
            (lens_hbm, lens_ref), (moves_hbm, moves_ref), (qkv_hbm.at[0], nat_ref.at[0]),
            (qkv_hbm.at[1], nat_ref.at[1]), (qkv_hbm.at[2], nat_ref.at[2]), (g_hbm, g_ref),
            (w_ref, w_all.at[pl.ds(pl.multiple_of(col * pad, 16), pad)])))
    ]
    for fetch in fetches:
        fetch.start()
    barrier = pltpu.get_barrier_semaphore()
    partners = [to_col(other_core), to_col(other_x), to_col(other_y)]
    partners += [to_rank(lax.rem(rank + k, n_dp)) for k in range(1, n_dp)]
    for partner in partners:
        pl.semaphore_signal(barrier, inc=1, device_id=partner, device_id_type=pl.DeviceIdType.MESH)
    pl.semaphore_wait(barrier, len(partners))

    def w_rows(owner, begin=0, count=pad):
        return w_all.at[pl.ds(pl.multiple_of(owner * pad + begin, 16), count)]

    def w_push(slot, src, owner, target, begin=0, count=pad):
        return push(src, w_rows(owner, begin, count), w_send.at[slot], w_recv.at[slot], to_col(target))

    started = []
    w_x = w_push(0, w_ref, col, other_x)
    w_y = w_push(1, w_ref, col, other_y)
    w_c = w_push(2, w_ref, col, other_core)
    started += [w_x, w_y, w_c]
    for fetch in fetches:
        fetch.wait()
    for i in range(3):
        qkv_ref[i] = nat_ref[i].T

    l0, l1, l2 = lens_ref[0, 0, rank], lens_ref[1, 0, rank], lens_ref[2, 0, rank]
    e0, e1 = l0, l0 + l1
    n_tok = g_ref.shape[0]

    def seg_of(places):
        return (places >= e0).astype(jnp.int32) + (places >= e1).astype(jnp.int32)

    allowed = seg_of(lax.broadcasted_iota(jnp.int32, (n_tok, n_tok), 0)) == seg_of(
        lax.broadcasted_iota(jnp.int32, (n_tok, n_tok), 1))
    gone = []
    for clip in range(3):
        flag = jnp.int32(0)
        for m in range(moves_ref.shape[1]):
            hit = jnp.logical_and(moves_ref[0, m, 0] == rank, moves_ref[0, m, 2] == clip)
            flag = jnp.where(hit, jnp.int32(1), flag)
        gone.append(flag)
    start, count = jnp.int32(0), jnp.int32(0)
    for m in range(moves_ref.shape[1]):
        mine, which = moves_ref[0, m, 0] == rank, moves_ref[0, m, 2]
        begin = jnp.where(which == 0, jnp.int32(0), jnp.where(which == 1, e0, e1))
        length = jnp.where(which == 0, l0, jnp.where(which == 1, l1, l2))
        start = jnp.where(mine, begin, start)
        count = jnp.where(mine, length, count)
    seg_row = seg_of(lax.broadcasted_iota(jnp.int32, (1, n_tok), 1))
    gone_row = jnp.where(seg_row == 0, gone[0], jnp.where(seg_row == 1, gone[1], gone[2]))
    stay_row = (1 - gone_row).astype(F32)
    pick_t = lax.broadcasted_iota(jnp.int32, (n_tok, CLIP_MAX), 0)
    pick_i = lax.broadcasted_iota(jnp.int32, (n_tok, CLIP_MAX), 1)
    picked = jnp.logical_and(pick_t == pick_i + start, pick_i < count)
    pick = jnp.where(picked, jnp.float32(1), jnp.float32(0)).astype(BF16)

    ahead = EARLY * pad
    succ = to_rank(lax.rem(rank + 1, n_dp))

    def e_push(slot, src, dst):
        copy = push(src, dst, e_send.at[slot], e_recv.at[slot], succ)
        started.append(copy)
        return copy

    early = []
    for i in range(3):
        early_out[i] = dot(qkv_ref[i, :ahead], pick, (1, 0)).astype(BF16)
        early.append(e_push(i, early_out.at[i], early_in.at[i]))

    pred = lax.rem(rank + n_dp - 1, n_dp)
    arriving = jnp.int32(0)
    for m in range(moves_ref.shape[1]):
        which = moves_ref[0, m, 2]
        length = jnp.where(which == 0, lens_ref[0, 0, pred], jnp.where(which == 1, lens_ref[1, 0, pred], lens_ref[2, 0, pred]))
        arriving = jnp.where(moves_ref[0, m, 1] == rank, length, arriving)
    box_allowed = lax.broadcasted_iota(jnp.int32, (CLIP_MAX, CLIP_MAX), 0) < arriving

    def softmax(scores, mask):
        scores = jnp.where(mask, scores, -1000000000.0)
        e = jnp.exp((scores - jnp.max(scores, axis=0, keepdims=True)) * HSIZE ** (-0.5))
        return (e * (1.0 / jnp.sum(e, axis=0, keepdims=True))).astype(BF16)

    def score_grad(p, dp):
        pf = p.astype(F32)
        ds = pf * (dp - jnp.sum(pf * dp, axis=0, keepdims=True))
        return (ds * HSIZE ** (-0.5)).astype(BF16)

    cot = g_ref[...]
    c_copies = []
    for h in range(HEADS):
        rows = pl.ds(h * pad, pad)
        q, k, v = qkv_ref[0, rows], nat_ref[1, :, h * pad:(h + 1) * pad], qkv_ref[2, rows]
        p = softmax(dot(k, q, (1, 0)), allowed)
        probs[h] = p
        mixed = dot(v, p, (1, 0)).astype(BF16)
        t_own[h % 2, h // 2] = dot(mixed, cot, (1, 0)).astype(BF16)
        if h % 2 == 1:
            m = h // 2
            c_copies.append(push(t_own.at[1 - core, m], t_core.at[m], c_send.at[m], c_recv.at[m], to_col(other_core)))
        if h == 3:
            w_x.wait_recv()
            diag_a = w_push(3, w_rows(other_x, 0, CUT), other_x, other_y, 0, CUT)
            pass_x = w_push(5, w_rows(other_x), other_x, other_core)
            w_y.wait_recv()
            diag_b = w_push(4, w_rows(other_y, CUT, pad - CUT), other_y, other_x, CUT, pad - CUT)
            pass_y = w_push(6, w_rows(other_y), other_y, other_core)
            started += [diag_a, pass_x, diag_b, pass_y]
    started += c_copies

    def r_push(slot, src, dst, target):
        copy = push(src, dst, r_send.at[slot], r_recv.at[slot], to_col(target))
        started.append(copy)
        return copy

    low, high = pl.ds(0, CUT), pl.ds(CUT, pad - CUT)
    for m in range(4):
        c_copies[m].wait_recv()
        chip[m] = (t_own[core, m].astype(F32) + t_core[m].astype(F32)).astype(BF16)
    to_x = [r_push(i, chip.at[2 * i + 1 - px, low], x_first.at[i], other_x) for i in range(2)]
    to_y = [r_push(2 + i, chip.at[2 * (1 - py) + i, high], y_first.at[i], other_y) for i in range(2)]

    diag_a.wait_recv()
    pass_a = w_push(7, w_rows(diagonal, 0, CUT), diagonal, other_core, 0, CUT)
    diag_b.wait_recv()
    pass_b = w_push(8, w_rows(diagonal, CUT, pad - CUT), diagonal, other_core, CUT, pad - CUT)
    started += [pass_a, pass_b]
    for copy in early:
        copy.wait_recv()
    for h in range(EARLY):
        rows = pl.ds(h * pad, pad)
        box_probs[h] = softmax(dot(early_in[1, rows], early_in[0, rows], (0, 0)), box_allowed)
    for copy in (w_c, pass_x, pass_y, pass_a, pass_b):
        copy.wait_recv()
    backs[...] = dot(w_all[...], cot, (1, 1)).astype(BF16)
    back_out[...] = dot(backs[:ahead], pick, (1, 0)).astype(BF16)
    ahead_back = e_push(3, back_out, back_in)

    boxes = []
    for at, h in enumerate(list(range(EARLY, HEADS)) + list(range(EARLY))):
        rows = pl.ds(h * pad, pad)
        q, k, v = qkv_ref[0, rows], qkv_ref[1, rows], nat_ref[2, :, h * pad:(h + 1) * pad]
        p, back = probs[h], backs[rows]
        ds = score_grad(p, dot(v, back, (1, 0)))
        grads = (dot(k, ds, (1, 0)), dot(q, ds, (1, 1)), dot(back, p, (1, 1)))
        for i, grad in enumerate(grads):
            home_t[i, rows] = (grad * stay_row).astype(BF16)
            if h >= EARLY:
                box_out[i, at] = dot(grad.astype(BF16), pick, (1, 0)).astype(BF16)
        if h >= EARLY:
            boxes.append(push(box_out.at[:, at], box_in.at[:, h], b_send.at[at], b_recv.at[at], succ))
        if at == 2:
            for i in range(2):
                to_x[i].wait_recv()
                x_mid[i] = (chip[2 * i + px, low].astype(F32) + x_first[i].astype(F32)).astype(BF16)
                to_y[i].wait_recv()
                y_mid[i] = (chip[2 * py + i, high].astype(F32) + y_first[i].astype(F32)).astype(BF16)
            then_y = r_push(4, x_mid.at[1 - py], y_last, other_y)
            then_x = r_push(5, y_mid.at[1 - px], x_last, other_x)
        if at == 5:
            then_y.wait_recv()
            then_x.wait_recv()
            own_low = x_mid[py].astype(F32) + y_last[...].astype(F32)
            own_high = y_mid[px].astype(F32) + x_last[...].astype(F32)
            width = z_out.shape[2]
            for part in range(n_dp):
                cut = slice(part * width, (part + 1) * width)
                z_out[part, low] = own_low[:, cut].astype(BF16)
                z_out[part, high] = own_high[:, cut].astype(BF16)
            z_copies = []
            for step in range(1, n_dp):
                target = lax.rem(rank + step, n_dp)
                z_copies.append(push(z_out.at[target], z_in.at[step - 1], z_send.at[step - 1], z_recv.at[step - 1], to_rank(target)))
    started += boxes + z_copies
    ahead_back.wait_recv()
    for h in range(EARLY):
        rows = pl.ds(h * pad, pad)
        q, k, v, back, p = early_in[0, rows], early_in[1, rows], early_in[2, rows], back_in[rows], box_probs[h]
        ds = score_grad(p, dot(v, back, (0, 0)))
        box_in[0, h] = dot(k, ds, (1, 0)).astype(BF16)
        box_in[1, h] = dot(q, ds, (1, 1)).astype(BF16)
        box_in[2, h] = dot(back, p, (1, 1)).astype(BF16)
    for i in range(3):
        home_ref[i] = home_t[i].T
    total = z_out[rank].astype(F32)
    for step, copy in enumerate(z_copies):
        copy.wait_recv()
        total += z_in[step].astype(F32)
    wg_ref[...] = total
    for copy in boxes:
        copy.wait_recv()
    for i in range(3):
        box_ref[i] = box_in[i].reshape(HEADS * pad, CLIP_MAX).T
    for copy in started:
        copy.wait_send()


def fused(qkv, grad_out, lengths, moves, out_weight):
    n_dp = lax.axis_size("dp")
    tok, feats = qkv.shape[2], qkv.shape[4]
    dout = grad_out.shape[3]
    pad, rest, width = HSIZE, HSIZE - CUT, dout // n_dp
    vmem = pl.BlockSpec(memory_space=pltpu.VMEM)
    hbm = pl.BlockSpec(memory_space=pltpu.HBM)
    natural = jnp.transpose(qkv[0, 0], (1, 0, 2))
    by_clip = jnp.transpose(lengths, (2, 1, 0))
    home, box, weight_grad = pl.pallas_call(
        block_kernel,
        out_shape=(
            jax.ShapeDtypeStruct((3, tok, feats), BF16),
            jax.ShapeDtypeStruct((3, CLIP_MAX, feats), BF16),
            jax.ShapeDtypeStruct((pad, width), F32),
        ),
        in_specs=[hbm] * 5,
        out_specs=(vmem, vmem, vmem),
        scratch_shapes=[
            pltpu.SMEM(by_clip.shape, jnp.int32),
            pltpu.SMEM(moves.shape, jnp.int32),
            pltpu.VMEM((3, tok, feats), BF16),
            pltpu.VMEM((3, feats, tok), BF16),
            pltpu.VMEM((tok, dout), BF16),
            pltpu.VMEM((3, feats, tok), BF16),
            pltpu.VMEM((3, HEADS, pad, CLIP_MAX), BF16),
            pltpu.VMEM((3, EARLY * pad, CLIP_MAX), BF16),
            pltpu.VMEM((3, EARLY * pad, CLIP_MAX), BF16),
            pltpu.VMEM((EARLY * pad, CLIP_MAX), BF16),
            pltpu.VMEM((EARLY * pad, CLIP_MAX), BF16),
            pltpu.VMEM((EARLY, CLIP_MAX, CLIP_MAX), BF16),
            pltpu.VMEM((feats, dout), BF16),
            pltpu.VMEM((HEADS, tok, tok), BF16),
            pltpu.VMEM((feats, tok), BF16),
            pltpu.VMEM((2, 4, pad, dout), BF16),
            pltpu.VMEM((4, pad, dout), BF16),
            pltpu.VMEM((4, pad, dout), BF16),
            pltpu.VMEM((2, CUT, dout), BF16),
            pltpu.VMEM((2, rest, dout), BF16),
            pltpu.VMEM((2, CUT, dout), BF16),
            pltpu.VMEM((2, rest, dout), BF16),
            pltpu.VMEM((rest, dout), BF16),
            pltpu.VMEM((CUT, dout), BF16),
            pltpu.VMEM((n_dp, pad, width), BF16),
            pltpu.VMEM((n_dp - 1, pad, width), BF16),
            pltpu.VMEM((3, HEADS - EARLY, pad, CLIP_MAX), BF16),
        ] + [pltpu.SemaphoreType.DMA((n,)) for n in (7, 9, 9, 4, 4, 6, 6, n_dp - 1, n_dp - 1, HEADS - EARLY, HEADS - EARLY, 4, 4)],
        compiler_params=pltpu.CompilerParams(
            collective_id=0, has_side_effects=True, vmem_limit_bytes=60 * 1024 * 1024
        ),
        name="block",
    )(by_clip, moves, natural, grad_out[0, 0], out_weight)
    home_grad = jnp.transpose(home, (1, 0, 2))
    inbox_grad = jnp.transpose(box, (1, 0, 2))
    return (home_grad[None, None], inbox_grad[None, None], weight_grad)


def solution(mesh):
    small = mesh.shape["dp"] == 4 and mesh.shape["fsdp"] == 8
    placed = (
        P("dp", "fsdp", None, None, None),
        P("dp", "fsdp", None, None),
        P(None, "fsdp", None),
        P("fsdp", None, None),
        P("fsdp", None),
    )
    return jax.shard_map(
        fused if small else local,
        mesh=mesh,
        in_specs=placed,
        out_specs=(
            P("dp", "fsdp", None, None, None),
            P("dp", "fsdp", None, None, None),
            P("fsdp", "dp"),
        ),
        check_vma=False,
    )
```

```python
import jax
import jax.numpy as jnp
from jax import lax
from jax.experimental import pallas as pl
from jax.experimental.pallas import tpu as pltpu
from jax.sharding import PartitionSpec as P

HEADS = 8
HSIZE = 112
TOK_DEV = 192
CLIP_MAX = 128


def passed_along(shard, axis, by):
    length = lax.axis_size(axis)
    return lax.ppermute(shard, axis, [(i, (i + by) % length) for i in range(length)])


def attend(rows, allowed, live):
    length = rows.shape[0]
    split = rows.reshape(length, 3, HEADS, HSIZE)
    queries = split[:, 0]
    keys = split[:, 1]
    values = split[:, 2]
    scores = jnp.einsum(
        "qhd,khd->hqk", queries, keys, preferred_element_type=jnp.float32
    ) * HSIZE ** (-0.5)
    scores = jnp.where(allowed[None], scores, -1000000000.0)
    probs = jax.nn.softmax(scores, axis=-1).astype(jnp.bfloat16)
    mixed = jnp.einsum("hqk,khd->qhd", probs, values, preferred_element_type=jnp.float32)
    mixed = jnp.where(live[:, None, None], mixed, 0.0)
    return mixed.reshape(length, HEADS * HSIZE).astype(jnp.bfloat16)


def clip_start(counts, which):
    starts = jnp.cumsum(counts) - counts
    clips = jnp.arange(counts.shape[0], dtype=jnp.int32)
    return (
        jnp.sum(jnp.where(clips == which, starts, 0)),
        jnp.sum(jnp.where(clips == which, counts, 0)),
    )


def home_masks(counts, moving, rank):
    ends = jnp.cumsum(counts)
    places = jnp.arange(TOK_DEV, dtype=jnp.int32)
    segment = jnp.sum((places[:, None] >= ends[None, :]).astype(jnp.int32), axis=1)
    clips = jnp.arange(counts.shape[0], dtype=jnp.int32)
    gone = jnp.any((moving[:, 0:1] == rank) & (moving[:, 2:3] == clips[None, :]), axis=0)
    stays = jnp.logical_not(jnp.any((segment[:, None] == clips[None, :]) & gone[None, :], axis=1))
    return (segment[:, None] == segment[None, :], stays)


def local(qkv, grad_out, lengths, moves, out_weight):
    home_rows = qkv[0, 0]
    home_cot = grad_out[0, 0]
    counts_all = lengths[:, 0]
    moving = moves[0]
    rank = lax.axis_index("dp")
    ranks = jnp.arange(counts_all.shape[0], dtype=jnp.int32)
    counts = jnp.sum(jnp.where((ranks == rank)[:, None], counts_all, 0), axis=0)
    allowed_home, stays = home_masks(counts, moving, rank)
    padded = jnp.concatenate(
        [home_rows, jnp.zeros((CLIP_MAX,) + home_rows.shape[1:], home_rows.dtype)], axis=0
    )
    cot_pad = jnp.concatenate(
        [home_cot, jnp.zeros((CLIP_MAX, home_cot.shape[1]), home_cot.dtype)], axis=0
    )
    send_off = jnp.zeros((), jnp.int32)
    sending = jnp.zeros((), jnp.bool_)
    box_len = jnp.zeros((), jnp.int32)
    receiving = jnp.zeros((), jnp.bool_)
    for step in range(moving.shape[0]):
        source = moving[step, 0]
        which = moving[step, 2]
        mine_out = source == rank
        offset, unused = clip_start(counts, which)
        send_off = jnp.where(mine_out, offset, send_off)
        sending = jnp.logical_or(sending, mine_out)
        source_counts = jnp.sum(jnp.where((ranks == source)[:, None], counts_all, 0), axis=0)
        ignored, length = clip_start(source_counts, which)
        mine_in = moving[step, 1] == rank
        box_len = jnp.where(mine_in, length, box_len)
        receiving = jnp.logical_or(receiving, mine_in)
    out_rows = jnp.where(
        sending,
        lax.dynamic_slice_in_dim(padded, send_off, CLIP_MAX, 0),
        jnp.zeros((), jnp.bfloat16),
    )
    out_cot = jnp.where(
        sending,
        lax.dynamic_slice_in_dim(cot_pad, send_off, CLIP_MAX, 0),
        jnp.zeros((), jnp.bfloat16),
    )
    got_rows, got_cot = passed_along((out_rows, out_cot), "dp", 1)
    box_rows = jnp.where(receiving, got_rows, jnp.zeros((), jnp.bfloat16))
    box_cot = jnp.where(receiving, got_cot, jnp.zeros((), jnp.bfloat16))
    places = jnp.arange(CLIP_MAX, dtype=jnp.int32)
    box_live = places < box_len
    box_allowed = jnp.broadcast_to(box_live[None, :], (CLIP_MAX, CLIP_MAX))

    def forward(home_in, box_in):
        return (attend(home_in, allowed_home, stays), attend(box_in, box_allowed, box_live))

    (mixed_home, mixed_box), pullback = jax.vjp(forward, home_rows, box_rows)
    weights = lax.all_gather(out_weight, "fsdp", axis=0, tiled=True)
    mixed_all = jnp.concatenate([mixed_home, mixed_box], axis=0)
    cot_all = jnp.concatenate([home_cot, box_cot], axis=0)
    back = lax.dot_general(
        cot_all, weights, (((1,), (1,)), ((), ())), preferred_element_type=jnp.float32
    ).astype(jnp.bfloat16)
    tokens_dev = home_rows.shape[0]
    grad_home, grad_box = pullback((back[:tokens_dev], back[tokens_dev:]))
    shard_rows = out_weight.shape[0]
    rank_sum = lax.psum_scatter(
        lax.dot_general(
            cot_all, mixed_all, (((0,), (0,)), ((), ())), preferred_element_type=jnp.float32
        ).astype(jnp.bfloat16),
        "dp",
        scatter_dimension=0,
        tiled=True,
    ).astype(jnp.float32)
    whole = lax.psum(rank_sum, "fsdp")
    piece = lax.dynamic_slice_in_dim(whole, lax.axis_index("fsdp") * shard_rows, shard_rows, 1)
    weight_grad = jnp.transpose(piece)
    return (grad_home[None, None], grad_box[None, None], weight_grad)


F32 = jnp.float32
BF16 = jnp.bfloat16
EARLY = 5
CUT = 64


def dot(a, b, dims):
    return lax.dot_general(a, b, ((dims[:1], dims[1:]), ((), ())), preferred_element_type=F32)


def block_kernel(
    lens_hbm, moves_hbm, qkv_hbm, g_hbm, w_ref,
    home_ref, box_ref, wg_ref,
    home_nat, box_nat, wg_own, lens_ref, moves_ref, nat_ref, qkv_ref, g_ref, home_t, box_in, early_out, early_in, back_out, back_in, box_probs, w_all, probs, backs, t_own, t_core, chip, x_first, y_first, x_mid, y_mid, x_last, y_last,
    z_out, z_in, box_out,
    in_sem, out_sem, w_send, w_recv, c_send, c_recv, r_send, r_recv, z_send, z_recv, b_send, b_recv, e_send, e_recv,
):
    rank, col = lax.axis_index("dp"), lax.axis_index("fsdp")
    core = lax.rem(col, 2)
    px = lax.rem(col // 2, 2)
    py = col // 4
    other_core = col + 1 - 2 * core
    other_x = col + 2 - 4 * px
    other_y = col + 4 - 8 * py
    diagonal = other_x + 4 - 8 * py
    n_dp = lax.axis_size("dp")
    pad = HSIZE

    def to_col(target):
        return {"dp": rank, "fsdp": target}

    def to_rank(target):
        return {"dp": target, "fsdp": col}

    def push(src, dst, send, recv, target):
        copy = pltpu.make_async_remote_copy(
            src_ref=src, dst_ref=dst, send_sem=send, recv_sem=recv,
            device_id=target, device_id_type=pl.DeviceIdType.MESH,
        )
        copy.start()
        return copy

    fetches = [
        pltpu.make_async_copy(src, dst, in_sem.at[i]) for i, (src, dst) in enumerate((
            (lens_hbm, lens_ref), (moves_hbm, moves_ref), (qkv_hbm.at[0], nat_ref.at[0]),
            (qkv_hbm.at[1], nat_ref.at[1]), (qkv_hbm.at[2], nat_ref.at[2]), (g_hbm, g_ref),
            (w_ref, w_all.at[pl.ds(pl.multiple_of(col * pad, 16), pad)])))
    ]
    for fetch in fetches:
        fetch.start()
    left = []

    def leave(slot, src, dst):
        copy = pltpu.make_async_copy(src, dst, out_sem.at[slot])
        copy.start()
        left.append(copy)

    barrier = pltpu.get_barrier_semaphore()
    partners = [to_col(other_core), to_col(other_x), to_col(other_y)]
    partners += [to_rank(lax.rem(rank + k, n_dp)) for k in range(1, n_dp)]
    for partner in partners:
        pl.semaphore_signal(barrier, inc=1, device_id=partner, device_id_type=pl.DeviceIdType.MESH)
    pl.semaphore_wait(barrier, len(partners))

    def w_rows(owner, begin=0, count=pad):
        return w_all.at[pl.ds(pl.multiple_of(owner * pad + begin, 16), count)]

    def w_push(slot, src, owner, target, begin=0, count=pad):
        return push(src, w_rows(owner, begin, count), w_send.at[slot], w_recv.at[slot], to_col(target))

    started = []
    w_x = w_push(0, w_ref, col, other_x)
    w_y = w_push(1, w_ref, col, other_y)
    w_c = w_push(2, w_ref, col, other_core)
    started += [w_x, w_y, w_c]
    for fetch in fetches:
        fetch.wait()
    for i in range(3):
        qkv_ref[i] = nat_ref[i].T

    l0, l1, l2 = lens_ref[0, 0, rank], lens_ref[1, 0, rank], lens_ref[2, 0, rank]
    e0, e1 = l0, l0 + l1
    n_tok = g_ref.shape[0]

    def seg_of(places):
        return (places >= e0).astype(jnp.int32) + (places >= e1).astype(jnp.int32)

    allowed = seg_of(lax.broadcasted_iota(jnp.int32, (n_tok, n_tok), 0)) == seg_of(
        lax.broadcasted_iota(jnp.int32, (n_tok, n_tok), 1))
    gone = []
    for clip in range(3):
        flag = jnp.int32(0)
        for m in range(moves_ref.shape[1]):
            hit = jnp.logical_and(moves_ref[0, m, 0] == rank, moves_ref[0, m, 2] == clip)
            flag = jnp.where(hit, jnp.int32(1), flag)
        gone.append(flag)
    start, count = jnp.int32(0), jnp.int32(0)
    for m in range(moves_ref.shape[1]):
        mine, which = moves_ref[0, m, 0] == rank, moves_ref[0, m, 2]
        begin = jnp.where(which == 0, jnp.int32(0), jnp.where(which == 1, e0, e1))
        length = jnp.where(which == 0, l0, jnp.where(which == 1, l1, l2))
        start = jnp.where(mine, begin, start)
        count = jnp.where(mine, length, count)
    seg_row = seg_of(lax.broadcasted_iota(jnp.int32, (1, n_tok), 1))
    gone_row = jnp.where(seg_row == 0, gone[0], jnp.where(seg_row == 1, gone[1], gone[2]))
    stay_row = (1 - gone_row).astype(F32)
    pick_t = lax.broadcasted_iota(jnp.int32, (n_tok, CLIP_MAX), 0)
    pick_i = lax.broadcasted_iota(jnp.int32, (n_tok, CLIP_MAX), 1)
    picked = jnp.logical_and(pick_t == pick_i + start, pick_i < count)
    pick = jnp.where(picked, jnp.float32(1), jnp.float32(0)).astype(BF16)

    ahead = EARLY * pad
    succ = to_rank(lax.rem(rank + 1, n_dp))

    def e_push(slot, src, dst):
        copy = push(src, dst, e_send.at[slot], e_recv.at[slot], succ)
        started.append(copy)
        return copy

    early = []
    for i in range(3):
        early_out[i] = dot(qkv_ref[i, :ahead], pick, (1, 0)).astype(BF16)
        early.append(e_push(i, early_out.at[i], early_in.at[i]))

    pred = lax.rem(rank + n_dp - 1, n_dp)
    arriving = jnp.int32(0)
    for m in range(moves_ref.shape[1]):
        which = moves_ref[0, m, 2]
        length = jnp.where(which == 0, lens_ref[0, 0, pred], jnp.where(which == 1, lens_ref[1, 0, pred], lens_ref[2, 0, pred]))
        arriving = jnp.where(moves_ref[0, m, 1] == rank, length, arriving)
    box_allowed = lax.broadcasted_iota(jnp.int32, (CLIP_MAX, CLIP_MAX), 0) < arriving

    def softmax(scores, mask):
        scores = jnp.where(mask, scores, -1000000000.0)
        e = jnp.exp((scores - jnp.max(scores, axis=0, keepdims=True)) * HSIZE ** (-0.5))
        return (e * (1.0 / jnp.sum(e, axis=0, keepdims=True))).astype(BF16)

    def score_grad(p, dp):
        pf = p.astype(F32)
        ds = pf * (dp - jnp.sum(pf * dp, axis=0, keepdims=True))
        return (ds * HSIZE ** (-0.5)).astype(BF16)

    cot = g_ref[...]
    c_copies = []
    for h in range(HEADS):
        rows = pl.ds(h * pad, pad)
        q, k, v = qkv_ref[0, rows], nat_ref[1, :, h * pad:(h + 1) * pad], qkv_ref[2, rows]
        p = softmax(dot(k, q, (1, 0)), allowed)
        probs[h] = p
        mixed = dot(v, p, (1, 0)).astype(BF16)
        if h % 2 == 0:
            even = mixed
        else:
            m = h // 2
            term = dot(jnp.concatenate([even, mixed], axis=0), cot, (1, 0)).astype(BF16)
            t_own[0, m], t_own[1, m] = term[:pad], term[pad:]
            c_copies.append(push(t_own.at[1 - core, m], t_core.at[m], c_send.at[m], c_recv.at[m], to_col(other_core)))
        if h == 1:
            w_x.wait_recv()
            diag_a = w_push(3, w_rows(other_x, 0, CUT), other_x, other_y, 0, CUT)
            pass_x = w_push(5, w_rows(other_x), other_x, other_core)
            w_y.wait_recv()
            diag_b = w_push(4, w_rows(other_y, CUT, pad - CUT), other_y, other_x, CUT, pad - CUT)
            pass_y = w_push(6, w_rows(other_y), other_y, other_core)
            started += [diag_a, pass_x, diag_b, pass_y]
        if h == 5:
            diag_a.wait_recv()
            pass_a = w_push(7, w_rows(diagonal, 0, CUT), diagonal, other_core, 0, CUT)
            diag_b.wait_recv()
            pass_b = w_push(8, w_rows(diagonal, CUT, pad - CUT), diagonal, other_core, CUT, pad - CUT)
            started += [pass_a, pass_b]
    started += c_copies

    def r_push(slot, src, dst, target):
        copy = push(src, dst, r_send.at[slot], r_recv.at[slot], to_col(target))
        started.append(copy)
        return copy

    for copy in (w_c, pass_x, pass_y, pass_a, pass_b):
        copy.wait_recv()
    backs[...] = dot(w_all[...], cot, (1, 1)).astype(BF16)
    back_out[...] = dot(backs[:ahead], pick, (1, 0)).astype(BF16)
    ahead_back = e_push(3, back_out, back_in)

    low, high = pl.ds(0, CUT), pl.ds(CUT, pad - CUT)
    for m in range(4):
        c_copies[m].wait_recv()
        chip[m] = (t_own[core, m].astype(F32) + t_core[m].astype(F32)).astype(BF16)
    to_x = [r_push(i, chip.at[2 * i + 1 - px, low], x_first.at[i], other_x) for i in range(2)]
    to_y = [r_push(2 + i, chip.at[2 * (1 - py) + i, high], y_first.at[i], other_y) for i in range(2)]

    boxes = []
    for at, h in enumerate(list(range(EARLY, HEADS)) + list(range(EARLY))):
        rows = pl.ds(h * pad, pad)
        q, k, v = qkv_ref[0, rows], qkv_ref[1, rows], nat_ref[2, :, h * pad:(h + 1) * pad]
        p, back = probs[h], backs[rows]
        ds = score_grad(p, dot(v, back, (1, 0)))
        grads = (dot(k, ds, (1, 0)), dot(q, ds, (1, 1)), dot(back, p, (1, 1)))
        if h >= EARLY:
            picked_grads = dot(jnp.concatenate([grad.astype(BF16) for grad in grads], axis=0), pick, (1, 0))
            for i in range(3):
                box_out[i, at] = picked_grads[i * pad:(i + 1) * pad].astype(BF16)
            boxes.append(push(box_out.at[:, at], box_in.at[:, h], b_send.at[at], b_recv.at[at], succ))
        for i, grad in enumerate(grads):
            home_t[i, rows] = (grad * stay_row).astype(BF16)
        if at == HEADS - EARLY - 1:
            for copy in early:
                copy.wait_recv()
            for b in range(EARLY):
                rows = pl.ds(b * pad, pad)
                box_probs[b] = softmax(dot(early_in[1, rows], early_in[0, rows], (0, 0)), box_allowed)
        if at == 4:
            for i in range(2):
                to_x[i].wait_recv()
                x_mid[i] = (chip[2 * i + px, low].astype(F32) + x_first[i].astype(F32)).astype(BF16)
                to_y[i].wait_recv()
                y_mid[i] = (chip[2 * py + i, high].astype(F32) + y_first[i].astype(F32)).astype(BF16)
            then_y = r_push(4, x_mid.at[1 - py], y_last, other_y)
            then_x = r_push(5, y_mid.at[1 - px], x_last, other_x)
        if at == 7:
            then_y.wait_recv()
            then_x.wait_recv()
            own_low = x_mid[py].astype(F32) + y_last[...].astype(F32)
            own_high = y_mid[px].astype(F32) + x_last[...].astype(F32)
            width = z_out.shape[2]
            for part in range(n_dp):
                cut = slice(part * width, (part + 1) * width)
                z_out[part, low] = own_low[:, cut].astype(BF16)
                z_out[part, high] = own_high[:, cut].astype(BF16)
            z_copies = []
            for step in range(1, n_dp):
                target = lax.rem(rank + step, n_dp)
                z_copies.append(push(z_out.at[target], z_in.at[step - 1], z_send.at[step - 1], z_recv.at[step - 1], to_rank(target)))
    started += boxes + z_copies
    for i in range(3):
        home_nat[i] = home_t[i].T
        leave(i, home_nat.at[i], home_ref.at[i])
    ahead_back.wait_recv()
    for h in range(EARLY):
        rows = pl.ds(h * pad, pad)
        q, k, v, back, p = early_in[0, rows], early_in[1, rows], early_in[2, rows], back_in[rows], box_probs[h]
        ds = score_grad(p, dot(v, back, (0, 0)))
        box_in[0, h] = dot(k, ds, (1, 0)).astype(BF16)
        box_in[1, h] = dot(q, ds, (1, 1)).astype(BF16)
        box_in[2, h] = dot(back, p, (1, 1)).astype(BF16)
    total = z_out[rank].astype(F32)
    for step, copy in enumerate(z_copies):
        copy.wait_recv()
        total += z_in[step].astype(F32)
    wg_own[...] = total
    leave(6, wg_own, wg_ref)
    for copy in boxes:
        copy.wait_recv()
    for i in range(3):
        box_nat[i] = box_in[i].reshape(HEADS * pad, CLIP_MAX).T
        leave(3 + i, box_nat.at[i], box_ref.at[i])
    for copy in left:
        copy.wait()
    for copy in started:
        copy.wait_send()


def hand_out(home, box, weight, home_to, box_to, weight_to, sem):
    copies = []
    for src, dst in ((home, home_to), (box, box_to)):
        half = src.shape[1] // 2
        for i in range(3):
            for begin in (0, half):
                at = (i, pl.ds(begin, half))
                copies.append(pltpu.make_async_copy(src.at[at], dst.at[at], sem.at[len(copies)]))
    copies.append(pltpu.make_async_copy(weight, weight_to, sem.at[len(copies)]))
    for copy in copies:
        copy.start()
    for copy in copies:
        copy.wait()


def fused(qkv, grad_out, lengths, moves, out_weight):
    n_dp = lax.axis_size("dp")
    tok, feats = qkv.shape[2], qkv.shape[4]
    dout = grad_out.shape[3]
    pad, rest, width = HSIZE, HSIZE - CUT, dout // n_dp
    hbm = pl.BlockSpec(memory_space=pltpu.HBM)
    natural = jnp.transpose(qkv[0, 0], (1, 0, 2))
    by_clip = jnp.transpose(lengths, (2, 1, 0))
    results = (
        jax.ShapeDtypeStruct((3, tok, feats), BF16),
        jax.ShapeDtypeStruct((3, CLIP_MAX, feats), BF16),
        jax.ShapeDtypeStruct((pad, width), F32),
    )
    made = pl.pallas_call(
        block_kernel,
        out_shape=results,
        in_specs=[hbm] * 5,
        out_specs=(hbm, hbm, hbm),
        scratch_shapes=[
            pltpu.VMEM((3, tok, feats), BF16),
            pltpu.VMEM((3, CLIP_MAX, feats), BF16),
            pltpu.VMEM((pad, width), F32),
            pltpu.SMEM(by_clip.shape, jnp.int32),
            pltpu.SMEM(moves.shape, jnp.int32),
            pltpu.VMEM((3, tok, feats), BF16),
            pltpu.VMEM((3, feats, tok), BF16),
            pltpu.VMEM((tok, dout), BF16),
            pltpu.VMEM((3, feats, tok), BF16),
            pltpu.VMEM((3, HEADS, pad, CLIP_MAX), BF16),
            pltpu.VMEM((3, EARLY * pad, CLIP_MAX), BF16),
            pltpu.VMEM((3, EARLY * pad, CLIP_MAX), BF16),
            pltpu.VMEM((EARLY * pad, CLIP_MAX), BF16),
            pltpu.VMEM((EARLY * pad, CLIP_MAX), BF16),
            pltpu.VMEM((EARLY, CLIP_MAX, CLIP_MAX), BF16),
            pltpu.VMEM((feats, dout), BF16),
            pltpu.VMEM((HEADS, tok, tok), BF16),
            pltpu.VMEM((feats, tok), BF16),
            pltpu.VMEM((2, 4, pad, dout), BF16),
            pltpu.VMEM((4, pad, dout), BF16),
            pltpu.VMEM((4, pad, dout), BF16),
            pltpu.VMEM((2, CUT, dout), BF16),
            pltpu.VMEM((2, rest, dout), BF16),
            pltpu.VMEM((2, CUT, dout), BF16),
            pltpu.VMEM((2, rest, dout), BF16),
            pltpu.VMEM((rest, dout), BF16),
            pltpu.VMEM((CUT, dout), BF16),
            pltpu.VMEM((n_dp, pad, width), BF16),
            pltpu.VMEM((n_dp - 1, pad, width), BF16),
            pltpu.VMEM((3, HEADS - EARLY, pad, CLIP_MAX), BF16),
        ] + [pltpu.SemaphoreType.DMA((n,)) for n in (7, 7, 9, 9, 4, 4, 6, 6, n_dp - 1, n_dp - 1, HEADS - EARLY, HEADS - EARLY, 4, 4)],
        compiler_params=pltpu.CompilerParams(
            collective_id=0, has_side_effects=True, vmem_limit_bytes=60 * 1024 * 1024
        ),
        name="block",
    )(by_clip, moves, natural, grad_out[0, 0], out_weight)
    home, box, weight_grad = pl.pallas_call(
        hand_out,
        out_shape=results,
        in_specs=[hbm] * 3,
        out_specs=(hbm,) * 3,
        scratch_shapes=[pltpu.SemaphoreType.DMA((13,))],
        compiler_params=pltpu.CompilerParams(vmem_limit_bytes=60 * 1024 * 1024),
        name="hand_out",
    )(*made)
    home_grad = jnp.transpose(home, (1, 0, 2))
    inbox_grad = jnp.transpose(box, (1, 0, 2))
    return (home_grad[None, None], inbox_grad[None, None], weight_grad)


def solution(mesh):
    small = mesh.shape["dp"] == 4 and mesh.shape["fsdp"] == 8
    placed = (
        P("dp", "fsdp", None, None, None),
        P("dp", "fsdp", None, None),
        P(None, "fsdp", None),
        P("fsdp", None, None),
        P("fsdp", None),
    )
    return jax.shard_map(
        fused if small else local,
        mesh=mesh,
        in_specs=placed,
        out_specs=(
            P("dp", "fsdp", None, None, None),
            P("dp", "fsdp", None, None, None),
            P("fsdp", "dp"),
        ),
        check_vma=False,
    )
```

```python
import jax
import jax.numpy as jnp
from jax import lax
from jax.experimental import pallas as pl
from jax.experimental.pallas import tpu as pltpu
from jax.sharding import PartitionSpec as P

HEADS = 8
HSIZE = 112
TOK_DEV = 192
CLIP_MAX = 128


def passed_along(shard, axis, by):
    length = lax.axis_size(axis)
    return lax.ppermute(shard, axis, [(i, (i + by) % length) for i in range(length)])


def attend(rows, allowed, live):
    length = rows.shape[0]
    split = rows.reshape(length, 3, HEADS, HSIZE)
    queries = split[:, 0]
    keys = split[:, 1]
    values = split[:, 2]
    scores = jnp.einsum(
        "qhd,khd->hqk", queries, keys, preferred_element_type=jnp.float32
    ) * HSIZE ** (-0.5)
    scores = jnp.where(allowed[None], scores, -1000000000.0)
    probs = jax.nn.softmax(scores, axis=-1).astype(jnp.bfloat16)
    mixed = jnp.einsum("hqk,khd->qhd", probs, values, preferred_element_type=jnp.float32)
    mixed = jnp.where(live[:, None, None], mixed, 0.0)
    return mixed.reshape(length, HEADS * HSIZE).astype(jnp.bfloat16)


def clip_start(counts, which):
    starts = jnp.cumsum(counts) - counts
    clips = jnp.arange(counts.shape[0], dtype=jnp.int32)
    return (
        jnp.sum(jnp.where(clips == which, starts, 0)),
        jnp.sum(jnp.where(clips == which, counts, 0)),
    )


def home_masks(counts, moving, rank):
    ends = jnp.cumsum(counts)
    places = jnp.arange(TOK_DEV, dtype=jnp.int32)
    segment = jnp.sum((places[:, None] >= ends[None, :]).astype(jnp.int32), axis=1)
    clips = jnp.arange(counts.shape[0], dtype=jnp.int32)
    gone = jnp.any((moving[:, 0:1] == rank) & (moving[:, 2:3] == clips[None, :]), axis=0)
    stays = jnp.logical_not(jnp.any((segment[:, None] == clips[None, :]) & gone[None, :], axis=1))
    return (segment[:, None] == segment[None, :], stays)


def local(qkv, grad_out, lengths, moves, out_weight):
    home_rows = qkv[0, 0]
    home_cot = grad_out[0, 0]
    counts_all = lengths[:, 0]
    moving = moves[0]
    rank = lax.axis_index("dp")
    ranks = jnp.arange(counts_all.shape[0], dtype=jnp.int32)
    counts = jnp.sum(jnp.where((ranks == rank)[:, None], counts_all, 0), axis=0)
    allowed_home, stays = home_masks(counts, moving, rank)
    padded = jnp.concatenate(
        [home_rows, jnp.zeros((CLIP_MAX,) + home_rows.shape[1:], home_rows.dtype)], axis=0
    )
    cot_pad = jnp.concatenate(
        [home_cot, jnp.zeros((CLIP_MAX, home_cot.shape[1]), home_cot.dtype)], axis=0
    )
    send_off = jnp.zeros((), jnp.int32)
    sending = jnp.zeros((), jnp.bool_)
    box_len = jnp.zeros((), jnp.int32)
    receiving = jnp.zeros((), jnp.bool_)
    for step in range(moving.shape[0]):
        source = moving[step, 0]
        which = moving[step, 2]
        mine_out = source == rank
        offset, unused = clip_start(counts, which)
        send_off = jnp.where(mine_out, offset, send_off)
        sending = jnp.logical_or(sending, mine_out)
        source_counts = jnp.sum(jnp.where((ranks == source)[:, None], counts_all, 0), axis=0)
        ignored, length = clip_start(source_counts, which)
        mine_in = moving[step, 1] == rank
        box_len = jnp.where(mine_in, length, box_len)
        receiving = jnp.logical_or(receiving, mine_in)
    out_rows = jnp.where(
        sending,
        lax.dynamic_slice_in_dim(padded, send_off, CLIP_MAX, 0),
        jnp.zeros((), jnp.bfloat16),
    )
    out_cot = jnp.where(
        sending,
        lax.dynamic_slice_in_dim(cot_pad, send_off, CLIP_MAX, 0),
        jnp.zeros((), jnp.bfloat16),
    )
    got_rows, got_cot = passed_along((out_rows, out_cot), "dp", 1)
    box_rows = jnp.where(receiving, got_rows, jnp.zeros((), jnp.bfloat16))
    box_cot = jnp.where(receiving, got_cot, jnp.zeros((), jnp.bfloat16))
    places = jnp.arange(CLIP_MAX, dtype=jnp.int32)
    box_live = places < box_len
    box_allowed = jnp.broadcast_to(box_live[None, :], (CLIP_MAX, CLIP_MAX))

    def forward(home_in, box_in):
        return (attend(home_in, allowed_home, stays), attend(box_in, box_allowed, box_live))

    (mixed_home, mixed_box), pullback = jax.vjp(forward, home_rows, box_rows)
    weights = lax.all_gather(out_weight, "fsdp", axis=0, tiled=True)
    mixed_all = jnp.concatenate([mixed_home, mixed_box], axis=0)
    cot_all = jnp.concatenate([home_cot, box_cot], axis=0)
    back = lax.dot_general(
        cot_all, weights, (((1,), (1,)), ((), ())), preferred_element_type=jnp.float32
    ).astype(jnp.bfloat16)
    tokens_dev = home_rows.shape[0]
    grad_home, grad_box = pullback((back[:tokens_dev], back[tokens_dev:]))
    shard_rows = out_weight.shape[0]
    rank_sum = lax.psum_scatter(
        lax.dot_general(
            cot_all, mixed_all, (((0,), (0,)), ((), ())), preferred_element_type=jnp.float32
        ).astype(jnp.bfloat16),
        "dp",
        scatter_dimension=0,
        tiled=True,
    ).astype(jnp.float32)
    whole = lax.psum(rank_sum, "fsdp")
    piece = lax.dynamic_slice_in_dim(whole, lax.axis_index("fsdp") * shard_rows, shard_rows, 1)
    weight_grad = jnp.transpose(piece)
    return (grad_home[None, None], grad_box[None, None], weight_grad)


F32 = jnp.float32
BF16 = jnp.bfloat16
EARLY = 5
CUT = 64


def dot(a, b, dims):
    return lax.dot_general(a, b, ((dims[:1], dims[1:]), ((), ())), preferred_element_type=F32)


def block_kernel(
    lens_hbm, moves_hbm, qkv_hbm, g_hbm, w_ref,
    home_ref, box_ref, wg_ref,
    lens_ref, moves_ref, nat_ref, qkv_ref, g_ref, home_t, box_in, early_out, early_in, back_out, back_in, box_probs, w_all, probs, backs, t_own, t_core, chip, x_first, y_first, x_mid, y_mid, x_last, y_last,
    z_out, z_in, box_out,
    in_sem, w_send, w_recv, c_send, c_recv, r_send, r_recv, z_send, z_recv, b_send, b_recv, e_send, e_recv,
):
    rank, col = lax.axis_index("dp"), lax.axis_index("fsdp")
    core = lax.rem(col, 2)
    px = lax.rem(col // 2, 2)
    py = col // 4
    other_core = col + 1 - 2 * core
    other_x = col + 2 - 4 * px
    other_y = col + 4 - 8 * py
    diagonal = other_x + 4 - 8 * py
    n_dp = lax.axis_size("dp")
    pad = HSIZE

    def to_col(target):
        return {"dp": rank, "fsdp": target}

    def to_rank(target):
        return {"dp": target, "fsdp": col}

    def push(src, dst, send, recv, target):
        copy = pltpu.make_async_remote_copy(
            src_ref=src, dst_ref=dst, send_sem=send, recv_sem=recv,
            device_id=target, device_id_type=pl.DeviceIdType.MESH,
        )
        copy.start()
        return copy

    fetches = [
        pltpu.make_async_copy(src, dst, in_sem.at[i]) for i, (src, dst) in enumerate((
            (lens_hbm, lens_ref), (moves_hbm, moves_ref), (qkv_hbm.at[0], nat_ref.at[0]),
            (qkv_hbm.at[1], nat_ref.at[1]), (qkv_hbm.at[2], nat_ref.at[2]), (g_hbm, g_ref),
            (w_ref, w_all.at[pl.ds(pl.multiple_of(col * pad, 16), pad)])))
    ]
    for fetch in fetches:
        fetch.start()
    barrier = pltpu.get_barrier_semaphore()
    partners = [to_col(other_core), to_col(other_x), to_col(other_y)]
    partners += [to_rank(lax.rem(rank + k, n_dp)) for k in range(1, n_dp)]
    for partner in partners:
        pl.semaphore_signal(barrier, inc=1, device_id=partner, device_id_type=pl.DeviceIdType.MESH)
    pl.semaphore_wait(barrier, len(partners))

    def w_rows(owner, begin=0, count=pad):
        return w_all.at[pl.ds(pl.multiple_of(owner * pad + begin, 16), count)]

    def w_push(slot, src, owner, target, begin=0, count=pad):
        return push(src, w_rows(owner, begin, count), w_send.at[slot], w_recv.at[slot], to_col(target))

    started = []
    w_x = w_push(0, w_ref, col, other_x)
    w_y = w_push(1, w_ref, col, other_y)
    w_c = w_push(2, w_ref, col, other_core)
    started += [w_x, w_y, w_c]
    for fetch in fetches:
        fetch.wait()
    for i in range(3):
        qkv_ref[i] = nat_ref[i].T

    l0, l1, l2 = lens_ref[0, 0, rank], lens_ref[1, 0, rank], lens_ref[2, 0, rank]
    e0, e1 = l0, l0 + l1
    n_tok = g_ref.shape[0]

    def seg_of(places):
        return (places >= e0).astype(jnp.int32) + (places >= e1).astype(jnp.int32)

    allowed = seg_of(lax.broadcasted_iota(jnp.int32, (n_tok, n_tok), 0)) == seg_of(
        lax.broadcasted_iota(jnp.int32, (n_tok, n_tok), 1))
    gone = []
    for clip in range(3):
        flag = jnp.int32(0)
        for m in range(moves_ref.shape[1]):
            hit = jnp.logical_and(moves_ref[0, m, 0] == rank, moves_ref[0, m, 2] == clip)
            flag = jnp.where(hit, jnp.int32(1), flag)
        gone.append(flag)
    start, count = jnp.int32(0), jnp.int32(0)
    for m in range(moves_ref.shape[1]):
        mine, which = moves_ref[0, m, 0] == rank, moves_ref[0, m, 2]
        begin = jnp.where(which == 0, jnp.int32(0), jnp.where(which == 1, e0, e1))
        length = jnp.where(which == 0, l0, jnp.where(which == 1, l1, l2))
        start = jnp.where(mine, begin, start)
        count = jnp.where(mine, length, count)
    seg_row = seg_of(lax.broadcasted_iota(jnp.int32, (1, n_tok), 1))
    gone_row = jnp.where(seg_row == 0, gone[0], jnp.where(seg_row == 1, gone[1], gone[2]))
    stay_row = (1 - gone_row).astype(F32)
    pick_t = lax.broadcasted_iota(jnp.int32, (n_tok, CLIP_MAX), 0)
    pick_i = lax.broadcasted_iota(jnp.int32, (n_tok, CLIP_MAX), 1)
    picked = jnp.logical_and(pick_t == pick_i + start, pick_i < count)
    pick = jnp.where(picked, jnp.float32(1), jnp.float32(0)).astype(BF16)

    ahead = EARLY * pad
    succ = to_rank(lax.rem(rank + 1, n_dp))

    def e_push(slot, src, dst):
        copy = push(src, dst, e_send.at[slot], e_recv.at[slot], succ)
        started.append(copy)
        return copy

    early = []
    for i in range(3):
        early_out[i] = dot(qkv_ref[i, :ahead], pick, (1, 0)).astype(BF16)
        early.append(e_push(i, early_out.at[i], early_in.at[i]))

    pred = lax.rem(rank + n_dp - 1, n_dp)
    arriving = jnp.int32(0)
    for m in range(moves_ref.shape[1]):
        which = moves_ref[0, m, 2]
        length = jnp.where(which == 0, lens_ref[0, 0, pred], jnp.where(which == 1, lens_ref[1, 0, pred], lens_ref[2, 0, pred]))
        arriving = jnp.where(moves_ref[0, m, 1] == rank, length, arriving)
    box_allowed = lax.broadcasted_iota(jnp.int32, (CLIP_MAX, CLIP_MAX), 0) < arriving

    def softmax(scores, mask):
        scores = jnp.where(mask, scores, -1000000000.0)
        e = jnp.exp((scores - jnp.max(scores, axis=0, keepdims=True)) * HSIZE ** (-0.5))
        return (e * (1.0 / jnp.sum(e, axis=0, keepdims=True))).astype(BF16)

    def score_grad(p, dp):
        pf = p.astype(F32)
        ds = pf * (dp - jnp.sum(pf * dp, axis=0, keepdims=True))
        return (ds * HSIZE ** (-0.5)).astype(BF16)

    cot = g_ref[...]
    c_copies = []
    for group in range(2):
        heads = [4 * group + i for i in range(4)]
        rows = [pl.ds(h * pad, pad) for h in heads]
        scores = [dot(nat_ref[1, :, h * pad:(h + 1) * pad], qkv_ref[0, rs], (1, 0)) for h, rs in zip(heads, rows)]
        ps = [softmax(each, allowed) for each in scores]
        mixed = [dot(qkv_ref[2, rs], p, (1, 0)).astype(BF16) for p, rs in zip(ps, rows)]
        for h, p in zip(heads, ps):
            probs[h] = p
        term = dot(jnp.concatenate(mixed, axis=0), cot, (1, 0)).astype(BF16)
        for i, h in enumerate(heads):
            t_own[h % 2, h // 2] = term[i * pad:(i + 1) * pad]
        for m in (2 * group, 2 * group + 1):
            c_copies.append(push(t_own.at[1 - core, m], t_core.at[m], c_send.at[m], c_recv.at[m], to_col(other_core)))
        if group == 0:
            w_x.wait_recv()
            diag_a = w_push(3, w_rows(other_x, 0, CUT), other_x, other_y, 0, CUT)
            pass_x = w_push(5, w_rows(other_x), other_x, other_core)
            w_y.wait_recv()
            diag_b = w_push(4, w_rows(other_y, CUT, pad - CUT), other_y, other_x, CUT, pad - CUT)
            pass_y = w_push(6, w_rows(other_y), other_y, other_core)
            started += [diag_a, pass_x, diag_b, pass_y]
    started += c_copies

    def r_push(slot, src, dst, target):
        copy = push(src, dst, r_send.at[slot], r_recv.at[slot], to_col(target))
        started.append(copy)
        return copy

    low, high = pl.ds(0, CUT), pl.ds(CUT, pad - CUT)
    for m in range(4):
        c_copies[m].wait_recv()
        chip[m] = (t_own[core, m].astype(F32) + t_core[m].astype(F32)).astype(BF16)
    to_x = [r_push(i, chip.at[2 * i + 1 - px, low], x_first.at[i], other_x) for i in range(2)]
    to_y = [r_push(2 + i, chip.at[2 * (1 - py) + i, high], y_first.at[i], other_y) for i in range(2)]

    diag_a.wait_recv()
    pass_a = w_push(7, w_rows(diagonal, 0, CUT), diagonal, other_core, 0, CUT)
    diag_b.wait_recv()
    pass_b = w_push(8, w_rows(diagonal, CUT, pad - CUT), diagonal, other_core, CUT, pad - CUT)
    started += [pass_a, pass_b]
    for copy in (w_c, pass_x, pass_y, pass_a, pass_b):
        copy.wait_recv()
    backs[...] = dot(w_all[...], cot, (1, 1)).astype(BF16)
    back_out[...] = dot(backs[:ahead], pick, (1, 0)).astype(BF16)
    ahead_back = e_push(3, back_out, back_in)

    def home_group(heads):
        rows = [pl.ds(h * pad, pad) for h in heads]
        ps = [probs[h] for h in heads]
        dps = [dot(nat_ref[2, :, h * pad:(h + 1) * pad], backs[rs], (1, 0)) for h, rs in zip(heads, rows)]
        dss = [score_grad(p, dp) for p, dp in zip(ps, dps)]
        grads = [
            (dot(qkv_ref[1, rs], ds, (1, 0)), dot(qkv_ref[0, rs], ds, (1, 1)), dot(backs[rs], p, (1, 1)))
            for rs, ds, p in zip(rows, dss, ps)
        ]
        for rs, each in zip(rows, grads):
            for i in range(3):
                home_t[i, rs] = (each[i] * stay_row).astype(BF16)
        return grads

    late = list(range(EARLY, HEADS))
    flat = [grad.astype(BF16) for each in home_group(late) for grad in each]
    picked_grads = dot(jnp.concatenate(flat, axis=0), pick, (1, 0)).astype(BF16)
    boxes = []
    for at, h in enumerate(late):
        for i in range(3):
            begin = (3 * at + i) * pad
            box_out[i, at] = picked_grads[begin:begin + pad]
        boxes.append(push(box_out.at[:, at], box_in.at[:, h], b_send.at[at], b_recv.at[at], succ))

    for copy in early:
        copy.wait_recv()
    clip_rows = [pl.ds(h * pad, pad) for h in range(EARLY)]
    clip_scores = [dot(early_in[1, rs], early_in[0, rs], (0, 0)) for rs in clip_rows]
    for h, each in enumerate(clip_scores):
        box_probs[h] = softmax(each, box_allowed)

    for i in range(2):
        to_x[i].wait_recv()
        x_mid[i] = (chip[2 * i + px, low].astype(F32) + x_first[i].astype(F32)).astype(BF16)
        to_y[i].wait_recv()
        y_mid[i] = (chip[2 * py + i, high].astype(F32) + y_first[i].astype(F32)).astype(BF16)
    then_y = r_push(4, x_mid.at[1 - py], y_last, other_y)
    then_x = r_push(5, y_mid.at[1 - px], x_last, other_x)

    home_group(list(range(EARLY)))

    then_y.wait_recv()
    then_x.wait_recv()
    own_low = x_mid[py].astype(F32) + y_last[...].astype(F32)
    own_high = y_mid[px].astype(F32) + x_last[...].astype(F32)
    width = z_out.shape[2]
    for part in range(n_dp):
        cut = slice(part * width, (part + 1) * width)
        z_out[part, low] = own_low[:, cut].astype(BF16)
        z_out[part, high] = own_high[:, cut].astype(BF16)
    z_copies = []
    for step in range(1, n_dp):
        target = lax.rem(rank + step, n_dp)
        z_copies.append(push(z_out.at[target], z_in.at[step - 1], z_send.at[step - 1], z_recv.at[step - 1], to_rank(target)))
    started += boxes + z_copies

    for i in range(3):
        home_ref[i] = home_t[i].T
    ahead_back.wait_recv()
    dps = [dot(early_in[2, rs], back_in[rs], (0, 0)) for rs in clip_rows]
    dss = [score_grad(box_probs[h], dps[h]) for h in range(EARLY)]
    for h, rs in enumerate(clip_rows):
        box_in[0, h] = dot(early_in[1, rs], dss[h], (1, 0)).astype(BF16)
        box_in[1, h] = dot(early_in[0, rs], dss[h], (1, 1)).astype(BF16)
        box_in[2, h] = dot(back_in[rs], box_probs[h], (1, 1)).astype(BF16)
    total = z_out[rank].astype(F32)
    for step, copy in enumerate(z_copies):
        copy.wait_recv()
        total += z_in[step].astype(F32)
    wg_ref[...] = total
    for copy in boxes:
        copy.wait_recv()
    for i in range(3):
        box_ref[i] = box_in[i].reshape(HEADS * pad, CLIP_MAX).T
    for copy in started:
        copy.wait_send()


def hand_out(home, box, weight, home_to, box_to, weight_to, sem):
    copies = []
    for src, dst in ((home, home_to), (box, box_to)):
        half = src.shape[1] // 2
        for i in range(3):
            for begin in (0, half):
                at = (i, pl.ds(begin, half))
                copies.append(pltpu.make_async_copy(src.at[at], dst.at[at], sem.at[len(copies)]))
    copies.append(pltpu.make_async_copy(weight, weight_to, sem.at[len(copies)]))
    for copy in copies:
        copy.start()
    for copy in copies:
        copy.wait()


def fused(qkv, grad_out, lengths, moves, out_weight):
    n_dp = lax.axis_size("dp")
    tok, feats = qkv.shape[2], qkv.shape[4]
    dout = grad_out.shape[3]
    pad, rest, width = HSIZE, HSIZE - CUT, dout // n_dp
    hbm = pl.BlockSpec(memory_space=pltpu.HBM)
    natural = jnp.transpose(qkv[0, 0], (1, 0, 2))
    by_clip = jnp.transpose(lengths, (2, 1, 0))
    vmem = pl.BlockSpec(memory_space=pltpu.VMEM)
    results = (
        jax.ShapeDtypeStruct((3, tok, feats), BF16),
        jax.ShapeDtypeStruct((3, CLIP_MAX, feats), BF16),
        jax.ShapeDtypeStruct((pad, width), F32),
    )
    made = pl.pallas_call(
        block_kernel,
        out_shape=tuple(pltpu.VMEM(each.shape, each.dtype) for each in results),
        in_specs=[hbm] * 5,
        out_specs=(vmem,) * 3,
        scratch_shapes=[
            pltpu.SMEM(by_clip.shape, jnp.int32),
            pltpu.SMEM(moves.shape, jnp.int32),
            pltpu.VMEM((3, tok, feats), BF16),
            pltpu.VMEM((3, feats, tok), BF16),
            pltpu.VMEM((tok, dout), BF16),
            pltpu.VMEM((3, feats, tok), BF16),
            pltpu.VMEM((3, HEADS, pad, CLIP_MAX), BF16),
            pltpu.VMEM((3, EARLY * pad, CLIP_MAX), BF16),
            pltpu.VMEM((3, EARLY * pad, CLIP_MAX), BF16),
            pltpu.VMEM((EARLY * pad, CLIP_MAX), BF16),
            pltpu.VMEM((EARLY * pad, CLIP_MAX), BF16),
            pltpu.VMEM((EARLY, CLIP_MAX, CLIP_MAX), BF16),
            pltpu.VMEM((feats, dout), BF16),
            pltpu.VMEM((HEADS, tok, tok), BF16),
            pltpu.VMEM((feats, tok), BF16),
            pltpu.VMEM((2, 4, pad, dout), BF16),
            pltpu.VMEM((4, pad, dout), BF16),
            pltpu.VMEM((4, pad, dout), BF16),
            pltpu.VMEM((2, CUT, dout), BF16),
            pltpu.VMEM((2, rest, dout), BF16),
            pltpu.VMEM((2, CUT, dout), BF16),
            pltpu.VMEM((2, rest, dout), BF16),
            pltpu.VMEM((rest, dout), BF16),
            pltpu.VMEM((CUT, dout), BF16),
            pltpu.VMEM((n_dp, pad, width), BF16),
            pltpu.VMEM((n_dp - 1, pad, width), BF16),
            pltpu.VMEM((3, HEADS - EARLY, pad, CLIP_MAX), BF16),
        ] + [pltpu.SemaphoreType.DMA((n,)) for n in (7, 9, 9, 4, 4, 6, 6, n_dp - 1, n_dp - 1, HEADS - EARLY, HEADS - EARLY, 4, 4)],
        compiler_params=pltpu.CompilerParams(
            collective_id=0, has_side_effects=True, vmem_limit_bytes=60 * 1024 * 1024
        ),
        name="block",
    )(by_clip, moves, natural, grad_out[0, 0], out_weight)
    home, box, weight_grad = pl.pallas_call(
        hand_out,
        out_shape=results,
        in_specs=[vmem] * 3,
        out_specs=(hbm,) * 3,
        scratch_shapes=[pltpu.SemaphoreType.DMA((13,))],
        compiler_params=pltpu.CompilerParams(vmem_limit_bytes=8 * 1024 * 1024),
        name="hand_out",
    )(*made)
    home_grad = jnp.transpose(home, (1, 0, 2))
    inbox_grad = jnp.transpose(box, (1, 0, 2))
    return (home_grad[None, None], inbox_grad[None, None], weight_grad)


def solution(mesh):
    small = mesh.shape["dp"] == 4 and mesh.shape["fsdp"] == 8
    placed = (
        P("dp", "fsdp", None, None, None),
        P("dp", "fsdp", None, None),
        P(None, "fsdp", None),
        P("fsdp", None, None),
        P("fsdp", None),
    )
    return jax.shard_map(
        fused if small else local,
        mesh=mesh,
        in_specs=placed,
        out_specs=(
            P("dp", "fsdp", None, None, None),
            P("dp", "fsdp", None, None, None),
            P("fsdp", "dp"),
        ),
        check_vma=False,
    )
```

```python
import jax
import jax.numpy as jnp
from jax import lax
from jax.experimental import pallas as pl
from jax.experimental.pallas import tpu as pltpu
from jax.sharding import PartitionSpec as P

HEADS = 8
HSIZE = 112
TOK_DEV = 192
CLIP_MAX = 128


def passed_along(shard, axis, by):
    length = lax.axis_size(axis)
    return lax.ppermute(shard, axis, [(i, (i + by) % length) for i in range(length)])


def attend(rows, allowed, live):
    length = rows.shape[0]
    split = rows.reshape(length, 3, HEADS, HSIZE)
    queries = split[:, 0]
    keys = split[:, 1]
    values = split[:, 2]
    scores = jnp.einsum(
        "qhd,khd->hqk", queries, keys, preferred_element_type=jnp.float32
    ) * HSIZE ** (-0.5)
    scores = jnp.where(allowed[None], scores, -1000000000.0)
    probs = jax.nn.softmax(scores, axis=-1).astype(jnp.bfloat16)
    mixed = jnp.einsum("hqk,khd->qhd", probs, values, preferred_element_type=jnp.float32)
    mixed = jnp.where(live[:, None, None], mixed, 0.0)
    return mixed.reshape(length, HEADS * HSIZE).astype(jnp.bfloat16)


def clip_start(counts, which):
    starts = jnp.cumsum(counts) - counts
    clips = jnp.arange(counts.shape[0], dtype=jnp.int32)
    return (
        jnp.sum(jnp.where(clips == which, starts, 0)),
        jnp.sum(jnp.where(clips == which, counts, 0)),
    )


def home_masks(counts, moving, rank):
    ends = jnp.cumsum(counts)
    places = jnp.arange(TOK_DEV, dtype=jnp.int32)
    segment = jnp.sum((places[:, None] >= ends[None, :]).astype(jnp.int32), axis=1)
    clips = jnp.arange(counts.shape[0], dtype=jnp.int32)
    gone = jnp.any((moving[:, 0:1] == rank) & (moving[:, 2:3] == clips[None, :]), axis=0)
    stays = jnp.logical_not(jnp.any((segment[:, None] == clips[None, :]) & gone[None, :], axis=1))
    return (segment[:, None] == segment[None, :], stays)


def local(qkv, grad_out, lengths, moves, out_weight):
    home_rows = qkv[0, 0]
    home_cot = grad_out[0, 0]
    counts_all = lengths[:, 0]
    moving = moves[0]
    rank = lax.axis_index("dp")
    ranks = jnp.arange(counts_all.shape[0], dtype=jnp.int32)
    counts = jnp.sum(jnp.where((ranks == rank)[:, None], counts_all, 0), axis=0)
    allowed_home, stays = home_masks(counts, moving, rank)
    padded = jnp.concatenate(
        [home_rows, jnp.zeros((CLIP_MAX,) + home_rows.shape[1:], home_rows.dtype)], axis=0
    )
    cot_pad = jnp.concatenate(
        [home_cot, jnp.zeros((CLIP_MAX, home_cot.shape[1]), home_cot.dtype)], axis=0
    )
    send_off = jnp.zeros((), jnp.int32)
    sending = jnp.zeros((), jnp.bool_)
    box_len = jnp.zeros((), jnp.int32)
    receiving = jnp.zeros((), jnp.bool_)
    for step in range(moving.shape[0]):
        source = moving[step, 0]
        which = moving[step, 2]
        mine_out = source == rank
        offset, unused = clip_start(counts, which)
        send_off = jnp.where(mine_out, offset, send_off)
        sending = jnp.logical_or(sending, mine_out)
        source_counts = jnp.sum(jnp.where((ranks == source)[:, None], counts_all, 0), axis=0)
        ignored, length = clip_start(source_counts, which)
        mine_in = moving[step, 1] == rank
        box_len = jnp.where(mine_in, length, box_len)
        receiving = jnp.logical_or(receiving, mine_in)
    out_rows = jnp.where(
        sending,
        lax.dynamic_slice_in_dim(padded, send_off, CLIP_MAX, 0),
        jnp.zeros((), jnp.bfloat16),
    )
    out_cot = jnp.where(
        sending,
        lax.dynamic_slice_in_dim(cot_pad, send_off, CLIP_MAX, 0),
        jnp.zeros((), jnp.bfloat16),
    )
    got_rows, got_cot = passed_along((out_rows, out_cot), "dp", 1)
    box_rows = jnp.where(receiving, got_rows, jnp.zeros((), jnp.bfloat16))
    box_cot = jnp.where(receiving, got_cot, jnp.zeros((), jnp.bfloat16))
    places = jnp.arange(CLIP_MAX, dtype=jnp.int32)
    box_live = places < box_len
    box_allowed = jnp.broadcast_to(box_live[None, :], (CLIP_MAX, CLIP_MAX))

    def forward(home_in, box_in):
        return (attend(home_in, allowed_home, stays), attend(box_in, box_allowed, box_live))

    (mixed_home, mixed_box), pullback = jax.vjp(forward, home_rows, box_rows)
    weights = lax.all_gather(out_weight, "fsdp", axis=0, tiled=True)
    mixed_all = jnp.concatenate([mixed_home, mixed_box], axis=0)
    cot_all = jnp.concatenate([home_cot, box_cot], axis=0)
    back = lax.dot_general(
        cot_all, weights, (((1,), (1,)), ((), ())), preferred_element_type=jnp.float32
    ).astype(jnp.bfloat16)
    tokens_dev = home_rows.shape[0]
    grad_home, grad_box = pullback((back[:tokens_dev], back[tokens_dev:]))
    shard_rows = out_weight.shape[0]
    rank_sum = lax.psum_scatter(
        lax.dot_general(
            cot_all, mixed_all, (((0,), (0,)), ((), ())), preferred_element_type=jnp.float32
        ).astype(jnp.bfloat16),
        "dp",
        scatter_dimension=0,
        tiled=True,
    ).astype(jnp.float32)
    whole = lax.psum(rank_sum, "fsdp")
    piece = lax.dynamic_slice_in_dim(whole, lax.axis_index("fsdp") * shard_rows, shard_rows, 1)
    weight_grad = jnp.transpose(piece)
    return (grad_home[None, None], grad_box[None, None], weight_grad)


F32 = jnp.float32
BF16 = jnp.bfloat16
EARLY = 5
CUT = 64


def dot(a, b, dims):
    return lax.dot_general(a, b, ((dims[:1], dims[1:]), ((), ())), preferred_element_type=F32)


def block_kernel(
    lens_hbm, moves_hbm, qkv_hbm, g_hbm, w_ref,
    home_ref, box_ref, wg_ref,
    lens_ref, moves_ref, nat_ref, qkv_ref, g_ref, home_t, box_in, early_out, early_in, back_out, back_in, box_probs, w_all, probs, backs, t_own, t_core, chip, x_first, y_first, x_mid, y_mid, x_last, y_last,
    z_out, z_in, box_out,
    in_sem, w_send, w_recv, c_send, c_recv, r_send, r_recv, z_send, z_recv, b_send, b_recv, e_send, e_recv,
):
    rank, col = lax.axis_index("dp"), lax.axis_index("fsdp")
    core = lax.rem(col, 2)
    px = lax.rem(col // 2, 2)
    py = col // 4
    other_core = col + 1 - 2 * core
    other_x = col + 2 - 4 * px
    other_y = col + 4 - 8 * py
    diagonal = other_x + 4 - 8 * py
    n_dp = lax.axis_size("dp")
    pad = HSIZE

    def to_col(target):
        return {"dp": rank, "fsdp": target}

    def to_rank(target):
        return {"dp": target, "fsdp": col}

    def push(src, dst, send, recv, target):
        copy = pltpu.make_async_remote_copy(
            src_ref=src, dst_ref=dst, send_sem=send, recv_sem=recv,
            device_id=target, device_id_type=pl.DeviceIdType.MESH,
        )
        copy.start()
        return copy

    fetches = [
        pltpu.make_async_copy(src, dst, in_sem.at[i]) for i, (src, dst) in enumerate((
            (lens_hbm, lens_ref), (moves_hbm, moves_ref), (qkv_hbm.at[0], nat_ref.at[0]),
            (qkv_hbm.at[1], nat_ref.at[1]), (qkv_hbm.at[2], nat_ref.at[2]), (g_hbm, g_ref),
            (w_ref, w_all.at[pl.ds(pl.multiple_of(col * pad, 16), pad)])))
    ]
    for fetch in fetches:
        fetch.start()
    barrier = pltpu.get_barrier_semaphore()
    partners = [to_col(other_core), to_col(other_x), to_col(other_y)]
    partners += [to_rank(lax.rem(rank + k, n_dp)) for k in range(1, n_dp)]
    for partner in partners:
        pl.semaphore_signal(barrier, inc=1, device_id=partner, device_id_type=pl.DeviceIdType.MESH)
    pl.semaphore_wait(barrier, len(partners))

    def w_rows(owner, begin=0, count=pad):
        return w_all.at[pl.ds(pl.multiple_of(owner * pad + begin, 16), count)]

    def w_push(slot, src, owner, target, begin=0, count=pad):
        return push(src, w_rows(owner, begin, count), w_send.at[slot], w_recv.at[slot], to_col(target))

    started = []
    rest = pad - CUT
    w_x = w_push(0, w_ref.at[pl.ds(0, CUT)], col, other_x, 0, CUT)
    w_y = w_push(1, w_ref.at[pl.ds(CUT, rest)], col, other_y, CUT, rest)
    w_x_rest = w_push(9, w_ref.at[pl.ds(CUT, rest)], col, other_x, CUT, rest)
    w_y_rest = w_push(10, w_ref.at[pl.ds(0, CUT)], col, other_y, 0, CUT)
    w_c = w_push(2, w_ref, col, other_core)
    started += [w_x, w_y, w_x_rest, w_y_rest, w_c]
    for fetch in fetches[:2]:
        fetch.wait()

    l0, l1, l2 = lens_ref[0, 0, rank], lens_ref[1, 0, rank], lens_ref[2, 0, rank]
    e0, e1 = l0, l0 + l1
    n_tok = g_ref.shape[0]

    def seg_of(places):
        return (places >= e0).astype(jnp.int32) + (places >= e1).astype(jnp.int32)

    allowed = seg_of(lax.broadcasted_iota(jnp.int32, (n_tok, n_tok), 0)) == seg_of(
        lax.broadcasted_iota(jnp.int32, (n_tok, n_tok), 1))
    gone = []
    for clip in range(3):
        flag = jnp.int32(0)
        for m in range(moves_ref.shape[1]):
            hit = jnp.logical_and(moves_ref[0, m, 0] == rank, moves_ref[0, m, 2] == clip)
            flag = jnp.where(hit, jnp.int32(1), flag)
        gone.append(flag)
    start, count = jnp.int32(0), jnp.int32(0)
    for m in range(moves_ref.shape[1]):
        mine, which = moves_ref[0, m, 0] == rank, moves_ref[0, m, 2]
        begin = jnp.where(which == 0, jnp.int32(0), jnp.where(which == 1, e0, e1))
        length = jnp.where(which == 0, l0, jnp.where(which == 1, l1, l2))
        start = jnp.where(mine, begin, start)
        count = jnp.where(mine, length, count)
    seg_row = seg_of(lax.broadcasted_iota(jnp.int32, (1, n_tok), 1))
    gone_row = jnp.where(seg_row == 0, gone[0], jnp.where(seg_row == 1, gone[1], gone[2]))
    stay_row = (1 - gone_row).astype(F32)
    pick_t = lax.broadcasted_iota(jnp.int32, (n_tok, CLIP_MAX), 0)
    pick_i = lax.broadcasted_iota(jnp.int32, (n_tok, CLIP_MAX), 1)
    picked = jnp.logical_and(pick_t == pick_i + start, pick_i < count)
    pick = jnp.where(picked, jnp.float32(1), jnp.float32(0)).astype(BF16)

    ahead = EARLY * pad
    succ = to_rank(lax.rem(rank + 1, n_dp))

    def e_push(slot, src, dst):
        copy = push(src, dst, e_send.at[slot], e_recv.at[slot], succ)
        started.append(copy)
        return copy

    early = []
    for i in range(3):
        fetches[2 + i].wait()
        qkv_ref[i] = nat_ref[i].T
        early_out[i] = dot(qkv_ref[i, :ahead], pick, (1, 0)).astype(BF16)
        early.append(e_push(i, early_out.at[i], early_in.at[i]))

    pred = lax.rem(rank + n_dp - 1, n_dp)
    arriving = jnp.int32(0)
    for m in range(moves_ref.shape[1]):
        which = moves_ref[0, m, 2]
        length = jnp.where(which == 0, lens_ref[0, 0, pred], jnp.where(which == 1, lens_ref[1, 0, pred], lens_ref[2, 0, pred]))
        arriving = jnp.where(moves_ref[0, m, 1] == rank, length, arriving)
    box_allowed = lax.broadcasted_iota(jnp.int32, (CLIP_MAX, CLIP_MAX), 0) < arriving

    def softmax(scores, mask):
        scores = jnp.where(mask, scores, -1000000000.0)
        e = jnp.exp((scores - jnp.max(scores, axis=0, keepdims=True)) * HSIZE ** (-0.5))
        return (e * (1.0 / jnp.sum(e, axis=0, keepdims=True))).astype(BF16)

    def score_grad(p, dp):
        pf = p.astype(F32)
        ds = pf * (dp - jnp.sum(pf * dp, axis=0, keepdims=True))
        return (ds * HSIZE ** (-0.5)).astype(BF16)

    for fetch in fetches[5:]:
        fetch.wait()
    cot = g_ref[...]
    c_copies = []
    for group in range(2):
        heads = [4 * group + i for i in range(4)]
        rows = [pl.ds(h * pad, pad) for h in heads]
        scores = [dot(nat_ref[1, :, h * pad:(h + 1) * pad], qkv_ref[0, rs], (1, 0)) for h, rs in zip(heads, rows)]
        ps = [softmax(each, allowed) for each in scores]
        mixed = [dot(qkv_ref[2, rs], p, (1, 0)).astype(BF16) for p, rs in zip(ps, rows)]
        for h, p in zip(heads, ps):
            probs[h] = p
        term = dot(jnp.concatenate(mixed, axis=0), cot, (1, 0)).astype(BF16)
        for i, h in enumerate(heads):
            t_own[h % 2, h // 2] = term[i * pad:(i + 1) * pad]
        for m in (2 * group, 2 * group + 1):
            c_copies.append(push(t_own.at[1 - core, m], t_core.at[m], c_send.at[m], c_recv.at[m], to_col(other_core)))
        if group == 0:
            w_x.wait_recv()
            diag_a = w_push(3, w_rows(other_x, 0, CUT), other_x, other_y, 0, CUT)
            w_y.wait_recv()
            diag_b = w_push(4, w_rows(other_y, CUT, rest), other_y, other_x, CUT, rest)
            started += [diag_a, diag_b]
    w_x_rest.wait_recv()
    pass_x = w_push(5, w_rows(other_x), other_x, other_core)
    w_y_rest.wait_recv()
    pass_y = w_push(6, w_rows(other_y), other_y, other_core)
    started += [pass_x, pass_y]
    started += c_copies

    def r_push(slot, src, dst, target):
        copy = push(src, dst, r_send.at[slot], r_recv.at[slot], to_col(target))
        started.append(copy)
        return copy

    low, high = pl.ds(0, CUT), pl.ds(CUT, pad - CUT)
    for m in range(4):
        c_copies[m].wait_recv()
        chip[m] = (t_own[core, m].astype(F32) + t_core[m].astype(F32)).astype(BF16)
    to_x = [r_push(i, chip.at[2 * i + 1 - px, low], x_first.at[i], other_x) for i in range(2)]
    to_y = [r_push(2 + i, chip.at[2 * (1 - py) + i, high], y_first.at[i], other_y) for i in range(2)]

    diag_a.wait_recv()
    pass_a = w_push(7, w_rows(diagonal, 0, CUT), diagonal, other_core, 0, CUT)
    diag_b.wait_recv()
    pass_b = w_push(8, w_rows(diagonal, CUT, pad - CUT), diagonal, other_core, CUT, pad - CUT)
    started += [pass_a, pass_b]
    for copy in (w_c, pass_x, pass_y, pass_a, pass_b):
        copy.wait_recv()
    backs[...] = dot(w_all[...], cot, (1, 1)).astype(BF16)
    back_out[...] = dot(backs[:ahead], pick, (1, 0)).astype(BF16)
    ahead_back = e_push(3, back_out, back_in)

    def home_group(heads):
        rows = [pl.ds(h * pad, pad) for h in heads]
        ps = [probs[h] for h in heads]
        dps = [dot(nat_ref[2, :, h * pad:(h + 1) * pad], backs[rs], (1, 0)) for h, rs in zip(heads, rows)]
        dss = [score_grad(p, dp) for p, dp in zip(ps, dps)]
        grads = [
            (dot(qkv_ref[1, rs], ds, (1, 0)), dot(qkv_ref[0, rs], ds, (1, 1)), dot(backs[rs], p, (1, 1)))
            for rs, ds, p in zip(rows, dss, ps)
        ]
        for rs, each in zip(rows, grads):
            for i in range(3):
                home_t[i, rs] = (each[i] * stay_row).astype(BF16)
        return grads

    late = list(range(EARLY, HEADS))
    flat = [grad.astype(BF16) for each in home_group(late) for grad in each]
    picked_grads = dot(jnp.concatenate(flat, axis=0), pick, (1, 0)).astype(BF16)
    boxes = []
    for at, h in enumerate(late):
        for i in range(3):
            begin = (3 * at + i) * pad
            box_out[i, at] = picked_grads[begin:begin + pad]
        boxes.append(push(box_out.at[:, at], box_in.at[:, h], b_send.at[at], b_recv.at[at], succ))

    for copy in early:
        copy.wait_recv()
    clip_rows = [pl.ds(h * pad, pad) for h in range(EARLY)]
    clip_scores = [dot(early_in[1, rs], early_in[0, rs], (0, 0)) for rs in clip_rows]
    for h, each in enumerate(clip_scores):
        box_probs[h] = softmax(each, box_allowed)

    for i in range(2):
        to_x[i].wait_recv()
        x_mid[i] = (chip[2 * i + px, low].astype(F32) + x_first[i].astype(F32)).astype(BF16)
        to_y[i].wait_recv()
        y_mid[i] = (chip[2 * py + i, high].astype(F32) + y_first[i].astype(F32)).astype(BF16)
    then_y = r_push(4, x_mid.at[1 - py], y_last, other_y)
    then_x = r_push(5, y_mid.at[1 - px], x_last, other_x)

    home_group(list(range(EARLY)))

    then_y.wait_recv()
    then_x.wait_recv()
    own_low = x_mid[py].astype(F32) + y_last[...].astype(F32)
    own_high = y_mid[px].astype(F32) + x_last[...].astype(F32)
    width = z_out.shape[2]
    for part in range(n_dp):
        cut = slice(part * width, (part + 1) * width)
        z_out[part, low] = own_low[:, cut].astype(BF16)
        z_out[part, high] = own_high[:, cut].astype(BF16)
    z_copies = []
    for step in range(1, n_dp):
        target = lax.rem(rank + step, n_dp)
        z_copies.append(push(z_out.at[target], z_in.at[step - 1], z_send.at[step - 1], z_recv.at[step - 1], to_rank(target)))
    started += boxes + z_copies

    for i in range(3):
        home_ref[i] = home_t[i].T
    ahead_back.wait_recv()
    dps = [dot(early_in[2, rs], back_in[rs], (0, 0)) for rs in clip_rows]
    dss = [score_grad(box_probs[h], dps[h]) for h in range(EARLY)]
    for h, rs in enumerate(clip_rows):
        box_in[0, h] = dot(early_in[1, rs], dss[h], (1, 0)).astype(BF16)
        box_in[1, h] = dot(early_in[0, rs], dss[h], (1, 1)).astype(BF16)
        box_in[2, h] = dot(back_in[rs], box_probs[h], (1, 1)).astype(BF16)
    for copy in boxes:
        copy.wait_recv()
    for i in range(3):
        box_ref[i] = box_in[i].reshape(HEADS * pad, CLIP_MAX).T
    total = z_out[rank].astype(F32)
    for step, copy in enumerate(z_copies):
        copy.wait_recv()
        total += z_in[step].astype(F32)
    wg_ref[...] = total
    for copy in started:
        copy.wait_send()


def hand_out(home, box, weight, home_to, box_to, weight_to, sem):
    copies = []
    for src, dst in ((home, home_to), (box, box_to)):
        half = src.shape[1] // 2
        for i in range(3):
            for begin in (0, half):
                at = (i, pl.ds(begin, half))
                copies.append(pltpu.make_async_copy(src.at[at], dst.at[at], sem.at[len(copies)]))
    copies.append(pltpu.make_async_copy(weight, weight_to, sem.at[len(copies)]))
    for copy in copies:
        copy.start()
    for copy in copies:
        copy.wait()


def fused(qkv, grad_out, lengths, moves, out_weight):
    n_dp = lax.axis_size("dp")
    tok, feats = qkv.shape[2], qkv.shape[4]
    dout = grad_out.shape[3]
    pad, rest, width = HSIZE, HSIZE - CUT, dout // n_dp
    hbm = pl.BlockSpec(memory_space=pltpu.HBM)
    natural = jnp.transpose(qkv[0, 0], (1, 0, 2))
    by_clip = jnp.transpose(lengths, (2, 1, 0))
    vmem = pl.BlockSpec(memory_space=pltpu.VMEM)
    results = (
        jax.ShapeDtypeStruct((3, tok, feats), BF16),
        jax.ShapeDtypeStruct((3, CLIP_MAX, feats), BF16),
        jax.ShapeDtypeStruct((pad, width), F32),
    )
    made = pl.pallas_call(
        block_kernel,
        out_shape=tuple(pltpu.VMEM(each.shape, each.dtype) for each in results),
        in_specs=[hbm] * 5,
        out_specs=(vmem,) * 3,
        scratch_shapes=[
            pltpu.SMEM(by_clip.shape, jnp.int32),
            pltpu.SMEM(moves.shape, jnp.int32),
            pltpu.VMEM((3, tok, feats), BF16),
            pltpu.VMEM((3, feats, tok), BF16),
            pltpu.VMEM((tok, dout), BF16),
            pltpu.VMEM((3, feats, tok), BF16),
            pltpu.VMEM((3, HEADS, pad, CLIP_MAX), BF16),
            pltpu.VMEM((3, EARLY * pad, CLIP_MAX), BF16),
            pltpu.VMEM((3, EARLY * pad, CLIP_MAX), BF16),
            pltpu.VMEM((EARLY * pad, CLIP_MAX), BF16),
            pltpu.VMEM((EARLY * pad, CLIP_MAX), BF16),
            pltpu.VMEM((EARLY, CLIP_MAX, CLIP_MAX), BF16),
            pltpu.VMEM((feats, dout), BF16),
            pltpu.VMEM((HEADS, tok, tok), BF16),
            pltpu.VMEM((feats, tok), BF16),
            pltpu.VMEM((2, 4, pad, dout), BF16),
            pltpu.VMEM((4, pad, dout), BF16),
            pltpu.VMEM((4, pad, dout), BF16),
            pltpu.VMEM((2, CUT, dout), BF16),
            pltpu.VMEM((2, rest, dout), BF16),
            pltpu.VMEM((2, CUT, dout), BF16),
            pltpu.VMEM((2, rest, dout), BF16),
            pltpu.VMEM((rest, dout), BF16),
            pltpu.VMEM((CUT, dout), BF16),
            pltpu.VMEM((n_dp, pad, width), BF16),
            pltpu.VMEM((n_dp - 1, pad, width), BF16),
            pltpu.VMEM((3, HEADS - EARLY, pad, CLIP_MAX), BF16),
        ] + [pltpu.SemaphoreType.DMA((n,)) for n in (7, 11, 11, 4, 4, 6, 6, n_dp - 1, n_dp - 1, HEADS - EARLY, HEADS - EARLY, 4, 4)],
        compiler_params=pltpu.CompilerParams(
            collective_id=0, has_side_effects=True, vmem_limit_bytes=60 * 1024 * 1024
        ),
        name="block",
    )(by_clip, moves, natural, grad_out[0, 0], out_weight)
    home, box, weight_grad = pl.pallas_call(
        hand_out,
        out_shape=results,
        in_specs=[vmem] * 3,
        out_specs=(hbm,) * 3,
        scratch_shapes=[pltpu.SemaphoreType.DMA((13,))],
        compiler_params=pltpu.CompilerParams(vmem_limit_bytes=8 * 1024 * 1024),
        name="hand_out",
    )(*made)
    home_grad = jnp.transpose(home, (1, 0, 2))
    inbox_grad = jnp.transpose(box, (1, 0, 2))
    return (home_grad[None, None], inbox_grad[None, None], weight_grad)


def solution(mesh):
    small = mesh.shape["dp"] == 4 and mesh.shape["fsdp"] == 8
    placed = (
        P("dp", "fsdp", None, None, None),
        P("dp", "fsdp", None, None),
        P(None, "fsdp", None),
        P("fsdp", None, None),
        P("fsdp", None),
    )
    return jax.shard_map(
        fused if small else local,
        mesh=mesh,
        in_specs=placed,
        out_specs=(
            P("dp", "fsdp", None, None, None),
            P("dp", "fsdp", None, None, None),
            P("fsdp", "dp"),
        ),
        check_vma=False,
    )
```

```python
import jax
import jax.numpy as jnp
from jax import lax
from jax.experimental import pallas as pl
from jax.experimental.pallas import tpu as pltpu
from jax.sharding import PartitionSpec as P

HEADS = 8
HSIZE = 112
TOK_DEV = 192
CLIP_MAX = 128


def passed_along(shard, axis, by):
    length = lax.axis_size(axis)
    return lax.ppermute(shard, axis, [(i, (i + by) % length) for i in range(length)])


def attend(rows, allowed, live):
    length = rows.shape[0]
    split = rows.reshape(length, 3, HEADS, HSIZE)
    queries = split[:, 0]
    keys = split[:, 1]
    values = split[:, 2]
    scores = jnp.einsum(
        "qhd,khd->hqk", queries, keys, preferred_element_type=jnp.float32
    ) * HSIZE ** (-0.5)
    scores = jnp.where(allowed[None], scores, -1000000000.0)
    probs = jax.nn.softmax(scores, axis=-1).astype(jnp.bfloat16)
    mixed = jnp.einsum("hqk,khd->qhd", probs, values, preferred_element_type=jnp.float32)
    mixed = jnp.where(live[:, None, None], mixed, 0.0)
    return mixed.reshape(length, HEADS * HSIZE).astype(jnp.bfloat16)


def clip_start(counts, which):
    starts = jnp.cumsum(counts) - counts
    clips = jnp.arange(counts.shape[0], dtype=jnp.int32)
    return (
        jnp.sum(jnp.where(clips == which, starts, 0)),
        jnp.sum(jnp.where(clips == which, counts, 0)),
    )


def home_masks(counts, moving, rank):
    ends = jnp.cumsum(counts)
    places = jnp.arange(TOK_DEV, dtype=jnp.int32)
    segment = jnp.sum((places[:, None] >= ends[None, :]).astype(jnp.int32), axis=1)
    clips = jnp.arange(counts.shape[0], dtype=jnp.int32)
    gone = jnp.any((moving[:, 0:1] == rank) & (moving[:, 2:3] == clips[None, :]), axis=0)
    stays = jnp.logical_not(jnp.any((segment[:, None] == clips[None, :]) & gone[None, :], axis=1))
    return (segment[:, None] == segment[None, :], stays)


def local(qkv, grad_out, lengths, moves, out_weight):
    home_rows = qkv[0, 0]
    home_cot = grad_out[0, 0]
    counts_all = lengths[:, 0]
    moving = moves[0]
    rank = lax.axis_index("dp")
    ranks = jnp.arange(counts_all.shape[0], dtype=jnp.int32)
    counts = jnp.sum(jnp.where((ranks == rank)[:, None], counts_all, 0), axis=0)
    allowed_home, stays = home_masks(counts, moving, rank)
    padded = jnp.concatenate(
        [home_rows, jnp.zeros((CLIP_MAX,) + home_rows.shape[1:], home_rows.dtype)], axis=0
    )
    cot_pad = jnp.concatenate(
        [home_cot, jnp.zeros((CLIP_MAX, home_cot.shape[1]), home_cot.dtype)], axis=0
    )
    send_off = jnp.zeros((), jnp.int32)
    sending = jnp.zeros((), jnp.bool_)
    box_len = jnp.zeros((), jnp.int32)
    receiving = jnp.zeros((), jnp.bool_)
    for step in range(moving.shape[0]):
        source = moving[step, 0]
        which = moving[step, 2]
        mine_out = source == rank
        offset, unused = clip_start(counts, which)
        send_off = jnp.where(mine_out, offset, send_off)
        sending = jnp.logical_or(sending, mine_out)
        source_counts = jnp.sum(jnp.where((ranks == source)[:, None], counts_all, 0), axis=0)
        ignored, length = clip_start(source_counts, which)
        mine_in = moving[step, 1] == rank
        box_len = jnp.where(mine_in, length, box_len)
        receiving = jnp.logical_or(receiving, mine_in)
    out_rows = jnp.where(
        sending,
        lax.dynamic_slice_in_dim(padded, send_off, CLIP_MAX, 0),
        jnp.zeros((), jnp.bfloat16),
    )
    out_cot = jnp.where(
        sending,
        lax.dynamic_slice_in_dim(cot_pad, send_off, CLIP_MAX, 0),
        jnp.zeros((), jnp.bfloat16),
    )
    got_rows, got_cot = passed_along((out_rows, out_cot), "dp", 1)
    box_rows = jnp.where(receiving, got_rows, jnp.zeros((), jnp.bfloat16))
    box_cot = jnp.where(receiving, got_cot, jnp.zeros((), jnp.bfloat16))
    places = jnp.arange(CLIP_MAX, dtype=jnp.int32)
    box_live = places < box_len
    box_allowed = jnp.broadcast_to(box_live[None, :], (CLIP_MAX, CLIP_MAX))

    def forward(home_in, box_in):
        return (attend(home_in, allowed_home, stays), attend(box_in, box_allowed, box_live))

    (mixed_home, mixed_box), pullback = jax.vjp(forward, home_rows, box_rows)
    weights = lax.all_gather(out_weight, "fsdp", axis=0, tiled=True)
    mixed_all = jnp.concatenate([mixed_home, mixed_box], axis=0)
    cot_all = jnp.concatenate([home_cot, box_cot], axis=0)
    back = lax.dot_general(
        cot_all, weights, (((1,), (1,)), ((), ())), preferred_element_type=jnp.float32
    ).astype(jnp.bfloat16)
    tokens_dev = home_rows.shape[0]
    grad_home, grad_box = pullback((back[:tokens_dev], back[tokens_dev:]))
    shard_rows = out_weight.shape[0]
    rank_sum = lax.psum_scatter(
        lax.dot_general(
            cot_all, mixed_all, (((0,), (0,)), ((), ())), preferred_element_type=jnp.float32
        ).astype(jnp.bfloat16),
        "dp",
        scatter_dimension=0,
        tiled=True,
    ).astype(jnp.float32)
    whole = lax.psum(rank_sum, "fsdp")
    piece = lax.dynamic_slice_in_dim(whole, lax.axis_index("fsdp") * shard_rows, shard_rows, 1)
    weight_grad = jnp.transpose(piece)
    return (grad_home[None, None], grad_box[None, None], weight_grad)


F32 = jnp.float32
BF16 = jnp.bfloat16
EARLY = 4
CUT = 64


def dot(a, b, dims):
    return lax.dot_general(a, b, ((dims[:1], dims[1:]), ((), ())), preferred_element_type=F32)


def block_kernel(
    lens_hbm, moves_hbm, qkv_hbm, g_hbm, w_ref,
    home_ref, box_ref, wg_ref,
    lens_ref, moves_ref, nat_ref, qkv_ref, g_ref, home_t, box_in, early_out, early_in, back_out, back_in, box_probs, w_all, probs, backs, t_own, t_core, chip, x_first, y_first, x_mid, y_mid, x_last, y_last,
    z_out, z_in, box_out,
    in_sem, w_send, w_recv, c_send, c_recv, r_send, r_recv, z_send, z_recv, b_send, b_recv, e_send, e_recv,
):
    rank, col = lax.axis_index("dp"), lax.axis_index("fsdp")
    core = lax.rem(col, 2)
    px = lax.rem(col // 2, 2)
    py = col // 4
    other_core = col + 1 - 2 * core
    other_x = col + 2 - 4 * px
    other_y = col + 4 - 8 * py
    diagonal = other_x + 4 - 8 * py
    n_dp = lax.axis_size("dp")
    pad = HSIZE

    def to_col(target):
        return {"dp": rank, "fsdp": target}

    def to_rank(target):
        return {"dp": target, "fsdp": col}

    def push(src, dst, send, recv, target):
        copy = pltpu.make_async_remote_copy(
            src_ref=src, dst_ref=dst, send_sem=send, recv_sem=recv,
            device_id=target, device_id_type=pl.DeviceIdType.MESH,
        )
        copy.start()
        return copy

    fetches = [
        pltpu.make_async_copy(src, dst, in_sem.at[i]) for i, (src, dst) in enumerate((
            (lens_hbm, lens_ref), (moves_hbm, moves_ref), (qkv_hbm.at[0], nat_ref.at[0]),
            (qkv_hbm.at[1], nat_ref.at[1]), (qkv_hbm.at[2], nat_ref.at[2]), (g_hbm, g_ref),
            (w_ref, w_all.at[pl.ds(pl.multiple_of(col * pad, 16), pad)])))
    ]
    for fetch in fetches:
        fetch.start()
    barrier = pltpu.get_barrier_semaphore()
    partners = [to_col(other_core), to_col(other_x), to_col(other_y)]
    partners += [to_rank(lax.rem(rank + k, n_dp)) for k in range(1, n_dp)]
    for partner in partners:
        pl.semaphore_signal(barrier, inc=1, device_id=partner, device_id_type=pl.DeviceIdType.MESH)
    pl.semaphore_wait(barrier, len(partners))

    def w_rows(owner, begin=0, count=pad):
        return w_all.at[pl.ds(pl.multiple_of(owner * pad + begin, 16), count)]

    def w_push(slot, src, owner, target, begin=0, count=pad):
        return push(src, w_rows(owner, begin, count), w_send.at[slot], w_recv.at[slot], to_col(target))

    started = []
    rest = pad - CUT
    w_x = w_push(0, w_ref.at[pl.ds(0, CUT)], col, other_x, 0, CUT)
    w_y = w_push(1, w_ref.at[pl.ds(CUT, rest)], col, other_y, CUT, rest)
    w_x_rest = w_push(9, w_ref.at[pl.ds(CUT, rest)], col, other_x, CUT, rest)
    w_y_rest = w_push(10, w_ref.at[pl.ds(0, CUT)], col, other_y, 0, CUT)
    w_c = w_push(2, w_ref, col, other_core)
    started += [w_x, w_y, w_x_rest, w_y_rest, w_c]
    for fetch in fetches[:2]:
        fetch.wait()

    l0, l1, l2 = lens_ref[0, 0, rank], lens_ref[1, 0, rank], lens_ref[2, 0, rank]
    e0, e1 = l0, l0 + l1
    n_tok = g_ref.shape[0]

    def seg_of(places):
        return (places >= e0).astype(jnp.int32) + (places >= e1).astype(jnp.int32)

    allowed = seg_of(lax.broadcasted_iota(jnp.int32, (n_tok, n_tok), 0)) == seg_of(
        lax.broadcasted_iota(jnp.int32, (n_tok, n_tok), 1))
    gone = []
    for clip in range(3):
        flag = jnp.int32(0)
        for m in range(moves_ref.shape[1]):
            hit = jnp.logical_and(moves_ref[0, m, 0] == rank, moves_ref[0, m, 2] == clip)
            flag = jnp.where(hit, jnp.int32(1), flag)
        gone.append(flag)
    start, count = jnp.int32(0), jnp.int32(0)
    for m in range(moves_ref.shape[1]):
        mine, which = moves_ref[0, m, 0] == rank, moves_ref[0, m, 2]
        begin = jnp.where(which == 0, jnp.int32(0), jnp.where(which == 1, e0, e1))
        length = jnp.where(which == 0, l0, jnp.where(which == 1, l1, l2))
        start = jnp.where(mine, begin, start)
        count = jnp.where(mine, length, count)
    seg_row = seg_of(lax.broadcasted_iota(jnp.int32, (1, n_tok), 1))
    gone_row = jnp.where(seg_row == 0, gone[0], jnp.where(seg_row == 1, gone[1], gone[2]))
    stay_row = (1 - gone_row).astype(F32)
    pick_t = lax.broadcasted_iota(jnp.int32, (n_tok, CLIP_MAX), 0)
    pick_i = lax.broadcasted_iota(jnp.int32, (n_tok, CLIP_MAX), 1)
    picked = jnp.logical_and(pick_t == pick_i + start, pick_i < count)
    pick = jnp.where(picked, jnp.float32(1), jnp.float32(0)).astype(BF16)

    ahead = EARLY * pad
    succ = to_rank(lax.rem(rank + 1, n_dp))

    def e_push(slot, src, dst):
        copy = push(src, dst, e_send.at[slot], e_recv.at[slot], succ)
        started.append(copy)
        return copy

    early = []
    for i in range(3):
        fetches[2 + i].wait()
        qkv_ref[i] = nat_ref[i].T
        early_out[i] = dot(qkv_ref[i, :ahead], pick, (1, 0)).astype(BF16)
        early.append(e_push(i, early_out.at[i], early_in.at[i]))

    pred = lax.rem(rank + n_dp - 1, n_dp)
    arriving = jnp.int32(0)
    for m in range(moves_ref.shape[1]):
        which = moves_ref[0, m, 2]
        length = jnp.where(which == 0, lens_ref[0, 0, pred], jnp.where(which == 1, lens_ref[1, 0, pred], lens_ref[2, 0, pred]))
        arriving = jnp.where(moves_ref[0, m, 1] == rank, length, arriving)
    box_allowed = lax.broadcasted_iota(jnp.int32, (CLIP_MAX, CLIP_MAX), 0) < arriving

    def softmax(scores, mask):
        scores = jnp.where(mask, scores, -1000000000.0)
        e = jnp.exp((scores - jnp.max(scores, axis=0, keepdims=True)) * HSIZE ** (-0.5))
        return (e * (1.0 / jnp.sum(e, axis=0, keepdims=True))).astype(BF16)

    def score_grad(p, dp):
        pf = p.astype(F32)
        ds = pf * (dp - jnp.sum(pf * dp, axis=0, keepdims=True))
        return (ds * HSIZE ** (-0.5)).astype(BF16)

    for fetch in fetches[5:]:
        fetch.wait()
    cot = g_ref[...]
    c_copies = []
    for group in range(2):
        heads = [4 * group + i for i in range(4)]
        rows = [pl.ds(h * pad, pad) for h in heads]
        scores = [dot(nat_ref[1, :, h * pad:(h + 1) * pad], qkv_ref[0, rs], (1, 0)) for h, rs in zip(heads, rows)]
        ps = [softmax(each, allowed) for each in scores]
        mixed = [dot(qkv_ref[2, rs], p, (1, 0)).astype(BF16) for p, rs in zip(ps, rows)]
        for h, p in zip(heads, ps):
            probs[h] = p
        term = dot(jnp.concatenate(mixed, axis=0), cot, (1, 0)).astype(BF16)
        for i, h in enumerate(heads):
            t_own[h % 2, h // 2] = term[i * pad:(i + 1) * pad]
        for m in (2 * group, 2 * group + 1):
            c_copies.append(push(t_own.at[1 - core, m], t_core.at[m], c_send.at[m], c_recv.at[m], to_col(other_core)))
        if group == 0:
            w_x.wait_recv()
            diag_a = w_push(3, w_rows(other_x, 0, CUT), other_x, other_y, 0, CUT)
            w_y.wait_recv()
            diag_b = w_push(4, w_rows(other_y, CUT, rest), other_y, other_x, CUT, rest)
            started += [diag_a, diag_b]
    w_x_rest.wait_recv()
    pass_x = w_push(5, w_rows(other_x), other_x, other_core)
    w_y_rest.wait_recv()
    pass_y = w_push(6, w_rows(other_y), other_y, other_core)
    started += [pass_x, pass_y]
    started += c_copies

    def r_push(slot, src, dst, target):
        copy = push(src, dst, r_send.at[slot], r_recv.at[slot], to_col(target))
        started.append(copy)
        return copy

    low, high = pl.ds(0, CUT), pl.ds(CUT, pad - CUT)
    for m in range(4):
        c_copies[m].wait_recv()
        chip[m] = (t_own[core, m].astype(F32) + t_core[m].astype(F32)).astype(BF16)
    to_x = [r_push(i, chip.at[2 * i + 1 - px, low], x_first.at[i], other_x) for i in range(2)]
    to_y = [r_push(2 + i, chip.at[2 * (1 - py) + i, high], y_first.at[i], other_y) for i in range(2)]

    diag_a.wait_recv()
    pass_a = w_push(7, w_rows(diagonal, 0, CUT), diagonal, other_core, 0, CUT)
    diag_b.wait_recv()
    pass_b = w_push(8, w_rows(diagonal, CUT, pad - CUT), diagonal, other_core, CUT, pad - CUT)
    started += [pass_a, pass_b]
    for copy in (w_c, pass_x, pass_y, pass_a, pass_b):
        copy.wait_recv()
    first = dot(w_all[:ahead], cot, (1, 1)).astype(BF16)
    back_out[...] = dot(first, pick, (1, 0)).astype(BF16)
    ahead_back = e_push(3, back_out, back_in)
    backs[:ahead] = first
    backs[ahead:] = dot(w_all[ahead:], cot, (1, 1)).astype(BF16)

    def home_group(heads):
        rows = [pl.ds(h * pad, pad) for h in heads]
        ps = [probs[h] for h in heads]
        dps = [dot(nat_ref[2, :, h * pad:(h + 1) * pad], backs[rs], (1, 0)) for h, rs in zip(heads, rows)]
        dss = [score_grad(p, dp) for p, dp in zip(ps, dps)]
        grads = [
            (dot(qkv_ref[1, rs], ds, (1, 0)), dot(qkv_ref[0, rs], ds, (1, 1)), dot(backs[rs], p, (1, 1)))
            for rs, ds, p in zip(rows, dss, ps)
        ]
        for rs, each in zip(rows, grads):
            for i in range(3):
                home_t[i, rs] = (each[i] * stay_row).astype(BF16)
        return grads

    late = list(range(EARLY, HEADS))
    flat = [grad.astype(BF16) for each in home_group(late) for grad in each]
    picked_grads = dot(jnp.concatenate(flat, axis=0), pick, (1, 0)).astype(BF16)
    boxes = []
    for at, h in enumerate(late):
        for i in range(3):
            begin = (3 * at + i) * pad
            box_out[i, at] = picked_grads[begin:begin + pad]
        boxes.append(push(box_out.at[:, at], box_in.at[:, h], b_send.at[at], b_recv.at[at], succ))

    for copy in early:
        copy.wait_recv()
    clip_rows = [pl.ds(h * pad, pad) for h in range(EARLY)]
    clip_scores = [dot(early_in[1, rs], early_in[0, rs], (0, 0)) for rs in clip_rows]
    for h, each in enumerate(clip_scores):
        box_probs[h] = softmax(each, box_allowed)

    for i in range(2):
        to_x[i].wait_recv()
        x_mid[i] = (chip[2 * i + px, low].astype(F32) + x_first[i].astype(F32)).astype(BF16)
        to_y[i].wait_recv()
        y_mid[i] = (chip[2 * py + i, high].astype(F32) + y_first[i].astype(F32)).astype(BF16)
    then_y = r_push(4, x_mid.at[1 - py], y_last, other_y)
    then_x = r_push(5, y_mid.at[1 - px], x_last, other_x)

    home_group(list(range(EARLY)))

    then_y.wait_recv()
    then_x.wait_recv()
    own_low = x_mid[py].astype(F32) + y_last[...].astype(F32)
    own_high = y_mid[px].astype(F32) + x_last[...].astype(F32)
    width = z_out.shape[2]
    for part in range(n_dp):
        cut = slice(part * width, (part + 1) * width)
        z_out[part, low] = own_low[:, cut].astype(BF16)
        z_out[part, high] = own_high[:, cut].astype(BF16)
    z_copies = []
    for step in range(1, n_dp):
        target = lax.rem(rank + step, n_dp)
        z_copies.append(push(z_out.at[target], z_in.at[step - 1], z_send.at[step - 1], z_recv.at[step - 1], to_rank(target)))
    started += boxes + z_copies

    for i in range(3):
        home_ref[i] = home_t[i].T
    ahead_back.wait_recv()
    dps = [dot(early_in[2, rs], back_in[rs], (0, 0)) for rs in clip_rows]
    dss = [score_grad(box_probs[h], dps[h]) for h in range(EARLY)]
    for h, rs in enumerate(clip_rows):
        box_in[0, h] = dot(early_in[1, rs], dss[h], (1, 0)).astype(BF16)
        box_in[1, h] = dot(early_in[0, rs], dss[h], (1, 1)).astype(BF16)
        box_in[2, h] = dot(back_in[rs], box_probs[h], (1, 1)).astype(BF16)
    for copy in boxes:
        copy.wait_recv()
    for i in range(3):
        box_ref[i] = box_in[i].reshape(HEADS * pad, CLIP_MAX).T
    total = z_out[rank].astype(F32)
    for step, copy in enumerate(z_copies):
        copy.wait_recv()
        total += z_in[step].astype(F32)
    wg_ref[...] = total
    for copy in started:
        copy.wait_send()


def hand_out(home, box, weight, home_to, box_to, weight_to, sem):
    copies = []
    for src, dst in ((home, home_to), (box, box_to)):
        half = src.shape[1] // 2
        for i in range(3):
            for begin in (0, half):
                at = (i, pl.ds(begin, half))
                copies.append(pltpu.make_async_copy(src.at[at], dst.at[at], sem.at[len(copies)]))
    copies.append(pltpu.make_async_copy(weight, weight_to, sem.at[len(copies)]))
    for copy in copies:
        copy.start()
    for copy in copies:
        copy.wait()


def fused(qkv, grad_out, lengths, moves, out_weight):
    n_dp = lax.axis_size("dp")
    tok, feats = qkv.shape[2], qkv.shape[4]
    dout = grad_out.shape[3]
    pad, rest, width = HSIZE, HSIZE - CUT, dout // n_dp
    hbm = pl.BlockSpec(memory_space=pltpu.HBM)
    natural = jnp.transpose(qkv[0, 0], (1, 0, 2))
    by_clip = jnp.transpose(lengths, (2, 1, 0))
    vmem = pl.BlockSpec(memory_space=pltpu.VMEM)
    results = (
        jax.ShapeDtypeStruct((3, tok, feats), BF16),
        jax.ShapeDtypeStruct((3, CLIP_MAX, feats), BF16),
        jax.ShapeDtypeStruct((pad, width), F32),
    )
    made = pl.pallas_call(
        block_kernel,
        out_shape=tuple(pltpu.VMEM(each.shape, each.dtype) for each in results),
        in_specs=[hbm] * 5,
        out_specs=(vmem,) * 3,
        scratch_shapes=[
            pltpu.SMEM(by_clip.shape, jnp.int32),
            pltpu.SMEM(moves.shape, jnp.int32),
            pltpu.VMEM((3, tok, feats), BF16),
            pltpu.VMEM((3, feats, tok), BF16),
            pltpu.VMEM((tok, dout), BF16),
            pltpu.VMEM((3, feats, tok), BF16),
            pltpu.VMEM((3, HEADS, pad, CLIP_MAX), BF16),
            pltpu.VMEM((3, EARLY * pad, CLIP_MAX), BF16),
            pltpu.VMEM((3, EARLY * pad, CLIP_MAX), BF16),
            pltpu.VMEM((EARLY * pad, CLIP_MAX), BF16),
            pltpu.VMEM((EARLY * pad, CLIP_MAX), BF16),
            pltpu.VMEM((EARLY, CLIP_MAX, CLIP_MAX), BF16),
            pltpu.VMEM((feats, dout), BF16),
            pltpu.VMEM((HEADS, tok, tok), BF16),
            pltpu.VMEM((feats, tok), BF16),
            pltpu.VMEM((2, 4, pad, dout), BF16),
            pltpu.VMEM((4, pad, dout), BF16),
            pltpu.VMEM((4, pad, dout), BF16),
            pltpu.VMEM((2, CUT, dout), BF16),
            pltpu.VMEM((2, rest, dout), BF16),
            pltpu.VMEM((2, CUT, dout), BF16),
            pltpu.VMEM((2, rest, dout), BF16),
            pltpu.VMEM((rest, dout), BF16),
            pltpu.VMEM((CUT, dout), BF16),
            pltpu.VMEM((n_dp, pad, width), BF16),
            pltpu.VMEM((n_dp - 1, pad, width), BF16),
            pltpu.VMEM((3, HEADS - EARLY, pad, CLIP_MAX), BF16),
        ] + [pltpu.SemaphoreType.DMA((n,)) for n in (7, 11, 11, 4, 4, 6, 6, n_dp - 1, n_dp - 1, HEADS - EARLY, HEADS - EARLY, 4, 4)],
        compiler_params=pltpu.CompilerParams(
            collective_id=0, has_side_effects=True, vmem_limit_bytes=60 * 1024 * 1024
        ),
        name="block",
    )(by_clip, moves, natural, grad_out[0, 0], out_weight)
    home, box, weight_grad = pl.pallas_call(
        hand_out,
        out_shape=results,
        in_specs=[vmem] * 3,
        out_specs=(hbm,) * 3,
        scratch_shapes=[pltpu.SemaphoreType.DMA((13,))],
        compiler_params=pltpu.CompilerParams(vmem_limit_bytes=8 * 1024 * 1024),
        name="hand_out",
    )(*made)
    home_grad = jnp.transpose(home, (1, 0, 2))
    inbox_grad = jnp.transpose(box, (1, 0, 2))
    return (home_grad[None, None], inbox_grad[None, None], weight_grad)


def solution(mesh):
    small = mesh.shape["dp"] == 4 and mesh.shape["fsdp"] == 8
    placed = (
        P("dp", "fsdp", None, None, None),
        P("dp", "fsdp", None, None),
        P(None, "fsdp", None),
        P("fsdp", None, None),
        P("fsdp", None),
    )
    return jax.shard_map(
        fused if small else local,
        mesh=mesh,
        in_specs=placed,
        out_specs=(
            P("dp", "fsdp", None, None, None),
            P("dp", "fsdp", None, None, None),
            P("fsdp", "dp"),
        ),
        check_vma=False,
    )
```

```python
import jax
import jax.numpy as jnp
from jax import lax
from jax.experimental import pallas as pl
from jax.experimental.pallas import tpu as pltpu
from jax.sharding import PartitionSpec as P

HEADS = 8
HSIZE = 112
TOK_DEV = 192
CLIP_MAX = 128


def passed_along(shard, axis, by):
    length = lax.axis_size(axis)
    return lax.ppermute(shard, axis, [(i, (i + by) % length) for i in range(length)])


def attend(rows, allowed, live):
    length = rows.shape[0]
    split = rows.reshape(length, 3, HEADS, HSIZE)
    queries = split[:, 0]
    keys = split[:, 1]
    values = split[:, 2]
    scores = jnp.einsum(
        "qhd,khd->hqk", queries, keys, preferred_element_type=jnp.float32
    ) * HSIZE ** (-0.5)
    scores = jnp.where(allowed[None], scores, -1000000000.0)
    probs = jax.nn.softmax(scores, axis=-1).astype(jnp.bfloat16)
    mixed = jnp.einsum("hqk,khd->qhd", probs, values, preferred_element_type=jnp.float32)
    mixed = jnp.where(live[:, None, None], mixed, 0.0)
    return mixed.reshape(length, HEADS * HSIZE).astype(jnp.bfloat16)


def clip_start(counts, which):
    starts = jnp.cumsum(counts) - counts
    clips = jnp.arange(counts.shape[0], dtype=jnp.int32)
    return (
        jnp.sum(jnp.where(clips == which, starts, 0)),
        jnp.sum(jnp.where(clips == which, counts, 0)),
    )


def home_masks(counts, moving, rank):
    ends = jnp.cumsum(counts)
    places = jnp.arange(TOK_DEV, dtype=jnp.int32)
    segment = jnp.sum((places[:, None] >= ends[None, :]).astype(jnp.int32), axis=1)
    clips = jnp.arange(counts.shape[0], dtype=jnp.int32)
    gone = jnp.any((moving[:, 0:1] == rank) & (moving[:, 2:3] == clips[None, :]), axis=0)
    stays = jnp.logical_not(jnp.any((segment[:, None] == clips[None, :]) & gone[None, :], axis=1))
    return (segment[:, None] == segment[None, :], stays)


def local(qkv, grad_out, lengths, moves, out_weight):
    home_rows = qkv[0, 0]
    home_cot = grad_out[0, 0]
    counts_all = lengths[:, 0]
    moving = moves[0]
    rank = lax.axis_index("dp")
    ranks = jnp.arange(counts_all.shape[0], dtype=jnp.int32)
    counts = jnp.sum(jnp.where((ranks == rank)[:, None], counts_all, 0), axis=0)
    allowed_home, stays = home_masks(counts, moving, rank)
    padded = jnp.concatenate(
        [home_rows, jnp.zeros((CLIP_MAX,) + home_rows.shape[1:], home_rows.dtype)], axis=0
    )
    cot_pad = jnp.concatenate(
        [home_cot, jnp.zeros((CLIP_MAX, home_cot.shape[1]), home_cot.dtype)], axis=0
    )
    send_off = jnp.zeros((), jnp.int32)
    sending = jnp.zeros((), jnp.bool_)
    box_len = jnp.zeros((), jnp.int32)
    receiving = jnp.zeros((), jnp.bool_)
    for step in range(moving.shape[0]):
        source = moving[step, 0]
        which = moving[step, 2]
        mine_out = source == rank
        offset, unused = clip_start(counts, which)
        send_off = jnp.where(mine_out, offset, send_off)
        sending = jnp.logical_or(sending, mine_out)
        source_counts = jnp.sum(jnp.where((ranks == source)[:, None], counts_all, 0), axis=0)
        ignored, length = clip_start(source_counts, which)
        mine_in = moving[step, 1] == rank
        box_len = jnp.where(mine_in, length, box_len)
        receiving = jnp.logical_or(receiving, mine_in)
    out_rows = jnp.where(
        sending,
        lax.dynamic_slice_in_dim(padded, send_off, CLIP_MAX, 0),
        jnp.zeros((), jnp.bfloat16),
    )
    out_cot = jnp.where(
        sending,
        lax.dynamic_slice_in_dim(cot_pad, send_off, CLIP_MAX, 0),
        jnp.zeros((), jnp.bfloat16),
    )
    got_rows, got_cot = passed_along((out_rows, out_cot), "dp", 1)
    box_rows = jnp.where(receiving, got_rows, jnp.zeros((), jnp.bfloat16))
    box_cot = jnp.where(receiving, got_cot, jnp.zeros((), jnp.bfloat16))
    places = jnp.arange(CLIP_MAX, dtype=jnp.int32)
    box_live = places < box_len
    box_allowed = jnp.broadcast_to(box_live[None, :], (CLIP_MAX, CLIP_MAX))

    def forward(home_in, box_in):
        return (attend(home_in, allowed_home, stays), attend(box_in, box_allowed, box_live))

    (mixed_home, mixed_box), pullback = jax.vjp(forward, home_rows, box_rows)
    weights = lax.all_gather(out_weight, "fsdp", axis=0, tiled=True)
    mixed_all = jnp.concatenate([mixed_home, mixed_box], axis=0)
    cot_all = jnp.concatenate([home_cot, box_cot], axis=0)
    back = lax.dot_general(
        cot_all, weights, (((1,), (1,)), ((), ())), preferred_element_type=jnp.float32
    ).astype(jnp.bfloat16)
    tokens_dev = home_rows.shape[0]
    grad_home, grad_box = pullback((back[:tokens_dev], back[tokens_dev:]))
    shard_rows = out_weight.shape[0]
    rank_sum = lax.psum_scatter(
        lax.dot_general(
            cot_all, mixed_all, (((0,), (0,)), ((), ())), preferred_element_type=jnp.float32
        ).astype(jnp.bfloat16),
        "dp",
        scatter_dimension=0,
        tiled=True,
    ).astype(jnp.float32)
    whole = lax.psum(rank_sum, "fsdp")
    piece = lax.dynamic_slice_in_dim(whole, lax.axis_index("fsdp") * shard_rows, shard_rows, 1)
    weight_grad = jnp.transpose(piece)
    return (grad_home[None, None], grad_box[None, None], weight_grad)


F32 = jnp.float32
BF16 = jnp.bfloat16
EARLY = 5
CUT = 64


def dot(a, b, dims):
    return lax.dot_general(a, b, ((dims[:1], dims[1:]), ((), ())), preferred_element_type=F32)


def block_kernel(
    lens_hbm, moves_hbm, qkv_hbm, g_hbm, w_ref,
    home_ref, box_ref, wg_ref,
    lens_ref, moves_ref, nat_ref, qkv_ref, g_ref, home_t, box_in, early_out, early_in, back_out, back_in, box_probs, w_all, probs, backs, t_own, t_core, chip, x_first, y_first, x_mid, y_mid, x_last, y_last,
    z_out, z_in, box_out,
    in_sem, w_send, w_recv, c_send, c_recv, r_send, r_recv, z_send, z_recv, b_send, b_recv, e_send, e_recv,
):
    rank, col = lax.axis_index("dp"), lax.axis_index("fsdp")
    core = lax.rem(col, 2)
    px = lax.rem(col // 2, 2)
    py = col // 4
    other_core = col + 1 - 2 * core
    other_x = col + 2 - 4 * px
    other_y = col + 4 - 8 * py
    diagonal = other_x + 4 - 8 * py
    n_dp = lax.axis_size("dp")
    pad = HSIZE

    def to_col(target):
        return {"dp": rank, "fsdp": target}

    def to_rank(target):
        return {"dp": target, "fsdp": col}

    def push(src, dst, send, recv, target):
        copy = pltpu.make_async_remote_copy(
            src_ref=src, dst_ref=dst, send_sem=send, recv_sem=recv,
            device_id=target, device_id_type=pl.DeviceIdType.MESH,
        )
        copy.start()
        return copy

    fetches = [
        pltpu.make_async_copy(src, dst, in_sem.at[i]) for i, (src, dst) in enumerate((
            (lens_hbm, lens_ref), (moves_hbm, moves_ref), (qkv_hbm.at[0], nat_ref.at[0]),
            (qkv_hbm.at[1], nat_ref.at[1]), (qkv_hbm.at[2], nat_ref.at[2]), (g_hbm, g_ref),
            (w_ref, w_all.at[pl.ds(pl.multiple_of(col * pad, 16), pad)])))
    ]
    for fetch in fetches:
        fetch.start()
    barrier = pltpu.get_barrier_semaphore()
    partners = [to_col(other_core), to_col(other_x), to_col(other_y)]
    partners += [to_rank(lax.rem(rank + k, n_dp)) for k in range(1, n_dp)]
    for partner in partners:
        pl.semaphore_signal(barrier, inc=1, device_id=partner, device_id_type=pl.DeviceIdType.MESH)
    pl.semaphore_wait(barrier, len(partners))

    def w_rows(owner, begin=0, count=pad):
        return w_all.at[pl.ds(pl.multiple_of(owner * pad + begin, 16), count)]

    def w_push(slot, src, owner, target, begin=0, count=pad):
        return push(src, w_rows(owner, begin, count), w_send.at[slot], w_recv.at[slot], to_col(target))

    started = []
    rest = pad - CUT
    w_x = w_push(0, w_ref.at[pl.ds(0, CUT)], col, other_x, 0, CUT)
    w_y = w_push(1, w_ref.at[pl.ds(CUT, rest)], col, other_y, CUT, rest)
    w_x_rest = w_push(9, w_ref.at[pl.ds(CUT, rest)], col, other_x, CUT, rest)
    w_y_rest = w_push(10, w_ref.at[pl.ds(0, CUT)], col, other_y, 0, CUT)
    w_c = w_push(2, w_ref, col, other_core)
    started += [w_x, w_y, w_x_rest, w_y_rest, w_c]
    for fetch in fetches[:2]:
        fetch.wait()

    l0, l1, l2 = lens_ref[0, 0, rank], lens_ref[1, 0, rank], lens_ref[2, 0, rank]
    e0, e1 = l0, l0 + l1
    n_tok = g_ref.shape[0]

    def seg_of(places):
        return (places >= e0).astype(jnp.int32) + (places >= e1).astype(jnp.int32)

    allowed = seg_of(lax.broadcasted_iota(jnp.int32, (n_tok, n_tok), 0)) == seg_of(
        lax.broadcasted_iota(jnp.int32, (n_tok, n_tok), 1))
    gone = []
    for clip in range(3):
        flag = jnp.int32(0)
        for m in range(moves_ref.shape[1]):
            hit = jnp.logical_and(moves_ref[0, m, 0] == rank, moves_ref[0, m, 2] == clip)
            flag = jnp.where(hit, jnp.int32(1), flag)
        gone.append(flag)
    start, count = jnp.int32(0), jnp.int32(0)
    for m in range(moves_ref.shape[1]):
        mine, which = moves_ref[0, m, 0] == rank, moves_ref[0, m, 2]
        begin = jnp.where(which == 0, jnp.int32(0), jnp.where(which == 1, e0, e1))
        length = jnp.where(which == 0, l0, jnp.where(which == 1, l1, l2))
        start = jnp.where(mine, begin, start)
        count = jnp.where(mine, length, count)
    seg_row = seg_of(lax.broadcasted_iota(jnp.int32, (1, n_tok), 1))
    gone_row = jnp.where(seg_row == 0, gone[0], jnp.where(seg_row == 1, gone[1], gone[2]))
    stay_row = (1 - gone_row).astype(F32)
    pick_t = lax.broadcasted_iota(jnp.int32, (n_tok, CLIP_MAX), 0)
    pick_i = lax.broadcasted_iota(jnp.int32, (n_tok, CLIP_MAX), 1)
    picked = jnp.logical_and(pick_t == pick_i + start, pick_i < count)
    pick = jnp.where(picked, jnp.float32(1), jnp.float32(0)).astype(BF16)

    ahead = EARLY * pad
    succ = to_rank(lax.rem(rank + 1, n_dp))

    def e_push(slot, src, dst):
        copy = push(src, dst, e_send.at[slot], e_recv.at[slot], succ)
        started.append(copy)
        return copy

    early = []
    near = -(-ahead // 128) * 128
    for i in range(3):
        fetches[2 + i].wait()
        qkv_ref[i, :near] = nat_ref[i, :, :near].T
        early_out[i] = dot(qkv_ref[i, :ahead], pick, (1, 0)).astype(BF16)
        early.append(e_push(i, early_out.at[i], early_in.at[i]))

    pred = lax.rem(rank + n_dp - 1, n_dp)
    arriving = jnp.int32(0)
    for m in range(moves_ref.shape[1]):
        which = moves_ref[0, m, 2]
        length = jnp.where(which == 0, lens_ref[0, 0, pred], jnp.where(which == 1, lens_ref[1, 0, pred], lens_ref[2, 0, pred]))
        arriving = jnp.where(moves_ref[0, m, 1] == rank, length, arriving)
    box_allowed = lax.broadcasted_iota(jnp.int32, (CLIP_MAX, CLIP_MAX), 0) < arriving

    def softmax(scores, mask):
        scores = jnp.where(mask, scores, -1000000000.0)
        e = jnp.exp((scores - jnp.max(scores, axis=0, keepdims=True)) * HSIZE ** (-0.5))
        return (e * (1.0 / jnp.sum(e, axis=0, keepdims=True))).astype(BF16)

    def score_grad(p, dp):
        pf = p.astype(F32)
        ds = pf * (dp - jnp.sum(pf * dp, axis=0, keepdims=True))
        return (ds * HSIZE ** (-0.5)).astype(BF16)

    for i in range(3):
        qkv_ref[i, near:] = nat_ref[i, :, near:].T
    for fetch in fetches[5:]:
        fetch.wait()
    cot = g_ref[...]
    c_copies = []
    for group in range(2):
        heads = [4 * group + i for i in range(4)]
        rows = [pl.ds(h * pad, pad) for h in heads]
        scores = [dot(nat_ref[1, :, h * pad:(h + 1) * pad], qkv_ref[0, rs], (1, 0)) for h, rs in zip(heads, rows)]
        ps = [softmax(each, allowed) for each in scores]
        mixed = [dot(qkv_ref[2, rs], p, (1, 0)).astype(BF16) for p, rs in zip(ps, rows)]
        for h, p in zip(heads, ps):
            probs[h] = p
        term = dot(jnp.concatenate(mixed, axis=0), cot, (1, 0)).astype(BF16)
        for i, h in enumerate(heads):
            t_own[h % 2, h // 2] = term[i * pad:(i + 1) * pad]
        for m in (2 * group, 2 * group + 1):
            c_copies.append(push(t_own.at[1 - core, m], t_core.at[m], c_send.at[m], c_recv.at[m], to_col(other_core)))
        if group == 0:
            w_x.wait_recv()
            diag_a = w_push(3, w_rows(other_x, 0, CUT), other_x, other_y, 0, CUT)
            w_y.wait_recv()
            diag_b = w_push(4, w_rows(other_y, CUT, rest), other_y, other_x, CUT, rest)
            started += [diag_a, diag_b]
    w_x_rest.wait_recv()
    pass_x = w_push(5, w_rows(other_x), other_x, other_core)
    w_y_rest.wait_recv()
    pass_y = w_push(6, w_rows(other_y), other_y, other_core)
    started += [pass_x, pass_y]
    started += c_copies

    def r_push(slot, src, dst, target):
        copy = push(src, dst, r_send.at[slot], r_recv.at[slot], to_col(target))
        started.append(copy)
        return copy

    low, high = pl.ds(0, CUT), pl.ds(CUT, pad - CUT)
    for m in range(4):
        c_copies[m].wait_recv()
        chip[m] = (t_own[core, m].astype(F32) + t_core[m].astype(F32)).astype(BF16)
    to_x = [r_push(i, chip.at[2 * i + 1 - px, low], x_first.at[i], other_x) for i in range(2)]
    to_y = [r_push(2 + i, chip.at[2 * (1 - py) + i, high], y_first.at[i], other_y) for i in range(2)]

    diag_a.wait_recv()
    pass_a = w_push(7, w_rows(diagonal, 0, CUT), diagonal, other_core, 0, CUT)
    diag_b.wait_recv()
    pass_b = w_push(8, w_rows(diagonal, CUT, pad - CUT), diagonal, other_core, CUT, pad - CUT)
    started += [pass_a, pass_b]
    for copy in (w_c, pass_x, pass_y, pass_a, pass_b):
        copy.wait_recv()
    first = dot(w_all[:ahead], cot, (1, 1)).astype(BF16)
    back_out[...] = dot(first, pick, (1, 0)).astype(BF16)
    ahead_back = e_push(3, back_out, back_in)
    backs[:ahead] = first
    backs[ahead:] = dot(w_all[ahead:], cot, (1, 1)).astype(BF16)

    def home_group(heads):
        rows = [pl.ds(h * pad, pad) for h in heads]
        ps = [probs[h] for h in heads]
        dps = [dot(nat_ref[2, :, h * pad:(h + 1) * pad], backs[rs], (1, 0)) for h, rs in zip(heads, rows)]
        dss = [score_grad(p, dp) for p, dp in zip(ps, dps)]
        grads = [
            (dot(qkv_ref[1, rs], ds, (1, 0)), dot(qkv_ref[0, rs], ds, (1, 1)), dot(backs[rs], p, (1, 1)))
            for rs, ds, p in zip(rows, dss, ps)
        ]
        for rs, each in zip(rows, grads):
            for i in range(3):
                home_t[i, rs] = (each[i] * stay_row).astype(BF16)
        return grads

    late = list(range(EARLY, HEADS))
    flat = [grad.astype(BF16) for each in home_group(late) for grad in each]
    picked_grads = dot(jnp.concatenate(flat, axis=0), pick, (1, 0)).astype(BF16)
    boxes = []
    for at, h in enumerate(late):
        for i in range(3):
            begin = (3 * at + i) * pad
            box_out[i, at] = picked_grads[begin:begin + pad]
        boxes.append(push(box_out.at[:, at], box_in.at[:, h], b_send.at[at], b_recv.at[at], succ))

    for copy in early:
        copy.wait_recv()
    clip_rows = [pl.ds(h * pad, pad) for h in range(EARLY)]
    clip_scores = [dot(early_in[1, rs], early_in[0, rs], (0, 0)) for rs in clip_rows]
    for h, each in enumerate(clip_scores):
        box_probs[h] = softmax(each, box_allowed)

    for i in range(2):
        to_x[i].wait_recv()
        x_mid[i] = (chip[2 * i + px, low].astype(F32) + x_first[i].astype(F32)).astype(BF16)
        to_y[i].wait_recv()
        y_mid[i] = (chip[2 * py + i, high].astype(F32) + y_first[i].astype(F32)).astype(BF16)
    then_y = r_push(4, x_mid.at[1 - py], y_last, other_y)
    then_x = r_push(5, y_mid.at[1 - px], x_last, other_x)

    home_group(list(range(EARLY)))

    then_y.wait_recv()
    then_x.wait_recv()
    own_low = x_mid[py].astype(F32) + y_last[...].astype(F32)
    own_high = y_mid[px].astype(F32) + x_last[...].astype(F32)
    width = z_out.shape[2]
    for part in range(n_dp):
        cut = slice(part * width, (part + 1) * width)
        z_out[part, low] = own_low[:, cut].astype(BF16)
        z_out[part, high] = own_high[:, cut].astype(BF16)
    z_copies = []
    for step in range(1, n_dp):
        target = lax.rem(rank + step, n_dp)
        z_copies.append(push(z_out.at[target], z_in.at[step - 1], z_send.at[step - 1], z_recv.at[step - 1], to_rank(target)))
    started += boxes + z_copies

    for i in range(3):
        home_ref[i] = home_t[i].T
    ahead_back.wait_recv()
    dps = [dot(early_in[2, rs], back_in[rs], (0, 0)) for rs in clip_rows]
    dss = [score_grad(box_probs[h], dps[h]) for h in range(EARLY)]
    for h, rs in enumerate(clip_rows):
        box_in[0, h] = dot(early_in[1, rs], dss[h], (1, 0)).astype(BF16)
        box_in[1, h] = dot(early_in[0, rs], dss[h], (1, 1)).astype(BF16)
        box_in[2, h] = dot(back_in[rs], box_probs[h], (1, 1)).astype(BF16)
    for copy in boxes:
        copy.wait_recv()
    for i in range(3):
        box_ref[i] = box_in[i].reshape(HEADS * pad, CLIP_MAX).T
    total = z_out[rank].astype(F32)
    for step, copy in enumerate(z_copies):
        copy.wait_recv()
        total += z_in[step].astype(F32)
    wg_ref[...] = total
    for copy in started:
        copy.wait_send()


def hand_out(home, box, weight, home_to, box_to, weight_to, sem):
    copies = []
    for src, dst in ((home, home_to), (box, box_to)):
        half = src.shape[1] // 2
        for i in range(3):
            for begin in (0, half):
                at = (i, pl.ds(begin, half))
                copies.append(pltpu.make_async_copy(src.at[at], dst.at[at], sem.at[len(copies)]))
    copies.append(pltpu.make_async_copy(weight, weight_to, sem.at[len(copies)]))
    for copy in copies:
        copy.start()
    for copy in copies:
        copy.wait()


def fused(qkv, grad_out, lengths, moves, out_weight):
    n_dp = lax.axis_size("dp")
    tok, feats = qkv.shape[2], qkv.shape[4]
    dout = grad_out.shape[3]
    pad, rest, width = HSIZE, HSIZE - CUT, dout // n_dp
    hbm = pl.BlockSpec(memory_space=pltpu.HBM)
    natural = jnp.transpose(qkv[0, 0], (1, 0, 2))
    by_clip = jnp.transpose(lengths, (2, 1, 0))
    vmem = pl.BlockSpec(memory_space=pltpu.VMEM)
    results = (
        jax.ShapeDtypeStruct((3, tok, feats), BF16),
        jax.ShapeDtypeStruct((3, CLIP_MAX, feats), BF16),
        jax.ShapeDtypeStruct((pad, width), F32),
    )
    made = pl.pallas_call(
        block_kernel,
        out_shape=tuple(pltpu.VMEM(each.shape, each.dtype) for each in results),
        in_specs=[hbm] * 5,
        out_specs=(vmem,) * 3,
        scratch_shapes=[
            pltpu.SMEM(by_clip.shape, jnp.int32),
            pltpu.SMEM(moves.shape, jnp.int32),
            pltpu.VMEM((3, tok, feats), BF16),
            pltpu.VMEM((3, feats, tok), BF16),
            pltpu.VMEM((tok, dout), BF16),
            pltpu.VMEM((3, feats, tok), BF16),
            pltpu.VMEM((3, HEADS, pad, CLIP_MAX), BF16),
            pltpu.VMEM((3, EARLY * pad, CLIP_MAX), BF16),
            pltpu.VMEM((3, EARLY * pad, CLIP_MAX), BF16),
            pltpu.VMEM((EARLY * pad, CLIP_MAX), BF16),
            pltpu.VMEM((EARLY * pad, CLIP_MAX), BF16),
            pltpu.VMEM((EARLY, CLIP_MAX, CLIP_MAX), BF16),
            pltpu.VMEM((feats, dout), BF16),
            pltpu.VMEM((HEADS, tok, tok), BF16),
            pltpu.VMEM((feats, tok), BF16),
            pltpu.VMEM((2, 4, pad, dout), BF16),
            pltpu.VMEM((4, pad, dout), BF16),
            pltpu.VMEM((4, pad, dout), BF16),
            pltpu.VMEM((2, CUT, dout), BF16),
            pltpu.VMEM((2, rest, dout), BF16),
            pltpu.VMEM((2, CUT, dout), BF16),
            pltpu.VMEM((2, rest, dout), BF16),
            pltpu.VMEM((rest, dout), BF16),
            pltpu.VMEM((CUT, dout), BF16),
            pltpu.VMEM((n_dp, pad, width), BF16),
            pltpu.VMEM((n_dp - 1, pad, width), BF16),
            pltpu.VMEM((3, HEADS - EARLY, pad, CLIP_MAX), BF16),
        ] + [pltpu.SemaphoreType.DMA((n,)) for n in (7, 11, 11, 4, 4, 6, 6, n_dp - 1, n_dp - 1, HEADS - EARLY, HEADS - EARLY, 4, 4)],
        compiler_params=pltpu.CompilerParams(
            collective_id=0, has_side_effects=True, vmem_limit_bytes=60 * 1024 * 1024
        ),
        name="block",
    )(by_clip, moves, natural, grad_out[0, 0], out_weight)
    home, box, weight_grad = pl.pallas_call(
        hand_out,
        out_shape=results,
        in_specs=[vmem] * 3,
        out_specs=(hbm,) * 3,
        scratch_shapes=[pltpu.SemaphoreType.DMA((13,))],
        compiler_params=pltpu.CompilerParams(vmem_limit_bytes=8 * 1024 * 1024),
        name="hand_out",
    )(*made)
    home_grad = jnp.transpose(home, (1, 0, 2))
    inbox_grad = jnp.transpose(box, (1, 0, 2))
    return (home_grad[None, None], inbox_grad[None, None], weight_grad)


def solution(mesh):
    small = mesh.shape["dp"] == 4 and mesh.shape["fsdp"] == 8
    placed = (
        P("dp", "fsdp", None, None, None),
        P("dp", "fsdp", None, None),
        P(None, "fsdp", None),
        P("fsdp", None, None),
        P("fsdp", None),
    )
    return jax.shard_map(
        fused if small else local,
        mesh=mesh,
        in_specs=placed,
        out_specs=(
            P("dp", "fsdp", None, None, None),
            P("dp", "fsdp", None, None, None),
            P("fsdp", "dp"),
        ),
        check_vma=False,
    )
```
